512 devices in a mesh: section: 128 (over x, z, y_hi), ch: 4 (over y_lo, core).
Axes of the slice: x: 4, y: 4 (y_hi: 2, y_lo: 2; y = y_hi * 2 + y_lo), z: 16, core: 2. Of those that a mesh axis runs over, the one named last changes fastest.
Arguments:
- act_carried: bfloat16 [128, 1280, 384], P('section', 'ch'), may hold values from -6 to 6
- cot_carried: bfloat16 [128, 1280, 384], P('section', 'ch'), may hold values from -6 to 6
- entry_latent: bfloat16 [1280, 384], P('ch'), may hold values from -6 to 6
- reward_head: bfloat16 [1280, 384], P('ch'), may hold values from -6 to 6
- stored_inputs: bfloat16 [128, 2, 1280, 384], P('section', None, 'ch'), may hold values from -6 to 6
- skip_buffer: bfloat16 [128, 2, 1280, 384], P('section', None, 'ch'), may hold values from -6 to 6
- conv_weight: bfloat16 [128, 3, 1280, 1280], P('section', None, 'ch'), may hold values from -0.09375 to 0.09375
- time_gain: float32 [25, 1280], P(None, 'ch'), may hold values from 0.5 to 1.5
- plan: int32 [128, 2], P('section'), may hold values from 0 to 1
- timesteps: int32 [128, 2], P('section'), may hold values from 0 to 24
Outputs:
- act_out: bfloat16 [128, 1280, 384], P('section', 'ch')
- cot_out: bfloat16 [128, 1280, 384], P('section', 'ch')
- mirror_in: bfloat16 [128, 1280, 384], P('section', 'ch')
The draws below stay inside these ranges and needn't reach their ends.
All inputs are finite; a program needn't handle non-finite values.
Results may differ from the reference program's by a relative error of at most 0.0032.
Values may be sent and summed in bfloat16 or wider, within the bound.
No kernel may reach another device: no remote copies, remote signals or barrier semaphores. Data moves between devices by JAX's collectives and lax.ppermute only.
A program may use at most 64 MiB of HBM per device.

```python
import jax
import jax.numpy as jnp
from jax import lax

C = 1280
GROUPS = 32
CELLS = 64
SLOTS = 2
TSTEPS = 25
ROWS = 384
SECTIONS = 128


def plant(values, rng, least, top_value):
    index_at = [jax.random.randint(jax.random.fold_in(rng, axis), (), 0, length) for axis, length in enumerate(values.shape)]
    widest = values.shape.index(max(values.shape))
    beside = index_at[:widest] + [(index_at[widest] + 1) % values.shape[widest]] + index_at[widest + 1:]
    return values.at[tuple(index_at)].set(least).at[tuple(beside)].set(top_value)


def shard_levels(key, extent, cuts, smallest, high):
    factor_of, own = 1.0, jax.random.fold_in(key, 6)
    for position, shards_of in cuts:
        draws = jnp.exp(jax.random.uniform(jax.random.fold_in(own, position), (shards_of,), jnp.float32, smallest / len(cuts), high / len(cuts)))
        factor_of = factor_of * jnp.repeat(draws, extent[position] // shards_of).reshape([-1 if axis == position else 1 for axis in range(len(extent))])
    return factor_of


def bell_draw(stream_key, shape, width, reach, cuts=(), kind=jnp.bfloat16):
    gain = shard_levels(stream_key, shape, cuts, -0.22, 0.18) if cuts else 1.0
    entries = jax.random.normal(stream_key, shape, jnp.float32) * width * gain
    return jnp.minimum(jnp.maximum(entries, -reach), reach).astype(kind)


def setup_inputs(seed: int = 0) -> dict:
    splits = jax.random.split(jax.random.key(seed), 11)
    return {
        "act_carried": bell_draw(splits[0], (SECTIONS, C, ROWS), 1.0, 6.0, ((0, 128), (1, 4))),
        "cot_carried": bell_draw(splits[1], (SECTIONS, C, ROWS), 1.0, 6.0, ((0, 128), (1, 4))),
        "entry_latent": bell_draw(splits[2], (C, ROWS), 1.0, 6.0, ((0, 4),)),
        "reward_head": bell_draw(splits[3], (C, ROWS), 1.0, 6.0, ((0, 4),)),
        "stored_inputs": bell_draw(splits[4], (SECTIONS, SLOTS, C, ROWS), 1.0, 6.0, ((0, 128), (2, 4))),
        "skip_buffer": bell_draw(splits[5], (SECTIONS, SLOTS, C, ROWS), 1.0, 6.0, ((0, 128), (2, 4))),
        "conv_weight": bell_draw(splits[6], (SECTIONS, 3, C, C), (3 * C) ** -0.5, 0.09375, ((0, 128), (2, 4))),
        "time_gain": jnp.clip(1.0 + 0.1 * jax.random.normal(splits[7], (TSTEPS, C), jnp.float32), 0.5, 1.5),
        "plan": plant(jax.random.randint(splits[8], (SECTIONS, 2), 0, SLOTS), jax.random.fold_in(splits[8], 1), 0, SLOTS - 1).astype(jnp.int32),
        "timesteps": plant(jax.random.randint(splits[9], (SECTIONS, 2), 0, TSTEPS), jax.random.fold_in(splits[9], 1), 0, TSTEPS - 1).astype(jnp.int32),
    }


epsilon = 1e-05

def frame_shift(values, frames_by):
    step = frames_by * CELLS
    if step > 0:
        return jnp.concatenate([values[:, step:], jnp.zeros((values.shape[0], step), values.dtype)], 1)
    if step < 0:
        return jnp.concatenate([jnp.zeros((values.shape[0], -step), values.dtype), values[:, :step]], 1)
    return values

def normalize(values):
    grouped = values.reshape(values.shape[0] // (C // GROUPS), -1)
    average = lax.optimization_barrier(jnp.mean(grouped, axis=1, keepdims=True))
    centred = grouped - average
    spread = lax.optimization_barrier(jnp.mean(centred * centred, axis=1, keepdims=True))
    factor = lax.rsqrt(spread + epsilon)
    return ((centred * factor).reshape(values.shape), factor)

def norm_back(normed, factor, d_normed):
    normed_g = normed.reshape(factor.shape[0], -1)
    grad_g = d_normed.reshape(factor.shape[0], -1)
    result = factor * (grad_g - lax.optimization_barrier(jnp.mean(grad_g, axis=1, keepdims=True)) - normed_g * lax.optimization_barrier(jnp.mean(grad_g * normed_g, axis=1, keepdims=True)))
    return result.reshape(normed.shape)

def silu_slope(normed):
    sigmoid = jax.nn.sigmoid(normed)
    return sigmoid * (1.0 + normed * (1.0 - sigmoid))

def reference(act_carried, cot_carried, entry_latent, reward_head, stored_inputs, skip_buffer, conv_weight, time_gain, plan, timesteps):
    inputs = jnp.concatenate([entry_latent[None], act_carried[:-1]], 0)
    cotans = jnp.concatenate([cot_carried[1:], reward_head[None]], 0)

    def one_section(s):
        weight = conv_weight[s]
        x_in = inputs[s]
        cot_in = cotans[s]
        encoder = s < SECTIONS // 2
        gains = time_gain[timesteps[s]]
        slot_ids = plan[s]
        skip_fwd = skip_buffer[s, slot_ids[0]].astype(jnp.float32)
        skip_bwd = skip_buffer[s, slot_ids[1]].astype(jnp.float32)
        saved = stored_inputs[s, slot_ids[1]].astype(jnp.float32)
        normed, factor = normalize(x_in.astype(jnp.float32))
        acted = jax.nn.silu(normed).astype(jnp.bfloat16)
        conv_sum = jnp.zeros((C, ROWS), jnp.float32)
        for k in range(3):
            conv_sum = conv_sum + jnp.dot(weight[k].T, frame_shift(acted, k - 1), preferred_element_type=jnp.float32)
        added = jnp.where(encoder, jnp.zeros_like(skip_fwd), skip_fwd)
        act_out = (x_in.astype(jnp.float32) + conv_sum * gains[0][:, None] + added).astype(jnp.bfloat16)
        cot_total = cot_in.astype(jnp.float32) + jnp.where(encoder, skip_bwd, jnp.zeros_like(skip_bwd))
        scaled = (cot_total * gains[1][:, None]).astype(jnp.bfloat16)
        d_acted = jnp.zeros((C, ROWS), jnp.float32)
        for k in range(3):
            d_acted = d_acted + frame_shift(jnp.dot(weight[k], scaled, preferred_element_type=jnp.float32), 1 - k)
        saved_normed, saved_factor = normalize(saved)
        d_normed = d_acted * silu_slope(saved_normed)
        cot_out = (cot_total + norm_back(saved_normed, saved_factor, d_normed)).astype(jnp.bfloat16)
        sent = jnp.where(encoder, act_out, cot_in)
        return (act_out, cot_out, sent)
    acts, cots, sents = lax.map(one_section, jnp.arange(SECTIONS, dtype=jnp.int32))
    return (acts, cots, sents[::-1])
```

```python
import jax
import jax.numpy as jnp
from jax import lax
from jax.sharding import PartitionSpec as P

C = 1280
GROUPS = 32
CELLS = 64


epsilon = 1e-05


def shifted(block, axis, distance):
    devices = range(lax.axis_size(axis))
    route = [(i - distance, i) for i in devices if i - distance in devices]
    return lax.ppermute(block, axis, route)


def frame_shift(values, frames_by):
    step = frames_by * CELLS
    if step > 0:
        return jnp.concatenate(
            [values[:, step:], jnp.zeros((values.shape[0], step), values.dtype)], 1
        )
    if step < 0:
        return jnp.concatenate(
            [jnp.zeros((values.shape[0], -step), values.dtype), values[:, :step]], 1
        )
    return values


def normalize(values):
    grouped = values.reshape(values.shape[0] // (C // GROUPS), -1)
    average = jnp.mean(grouped, axis=1, keepdims=True)
    centred = grouped - average
    spread = jnp.mean(centred * centred, axis=1, keepdims=True)
    factor = lax.rsqrt(spread + epsilon)
    return ((centred * factor).reshape(values.shape), factor)


def norm_back(normed, factor, d_normed):
    normed_g = normed.reshape(factor.shape[0], -1)
    grad_g = d_normed.reshape(factor.shape[0], -1)
    result = factor * (
        grad_g
        - jnp.mean(grad_g, axis=1, keepdims=True)
        - normed_g * jnp.mean(grad_g * normed_g, axis=1, keepdims=True)
    )
    return result.reshape(normed.shape)


def silu_slope(normed):
    sigmoid = jax.nn.sigmoid(normed)
    return sigmoid * (1.0 + normed * (1.0 - sigmoid))


def swap_core(block):
    return lax.ppermute(block, "ch", [(0, 1), (1, 0), (2, 3), (3, 2)])


def swap_chip(block):
    return lax.ppermute(block, "ch", [(0, 2), (2, 0), (1, 3), (3, 1)])


def pick(pair, index, axis):
    return lax.dynamic_index_in_dim(pair, index, axis, False)


def local(
    act_carried,
    cot_carried,
    entry_latent,
    reward_head,
    stored_inputs,
    skip_buffer,
    conv_weight,
    time_gain,
    plan,
    timesteps,
):
    sections = lax.axis_size("section")
    section_place = lax.axis_index("section")
    place = lax.axis_index("ch")
    core = place % 2
    chip = place // 2
    rows = act_carried.shape[1]
    weight = conv_weight[0]
    encoder = section_place < sections // 2

    arrived = shifted(act_carried[0], "section", 1)

    x_in = jnp.where(section_place == 0, entry_latent, arrived)
    slot_ids = plan[0]
    stamps = timesteps[0]
    one_hot = (stamps[:, None] == lax.iota(jnp.int32, time_gain.shape[0])[None, :]).astype(
        jnp.float32
    )
    gains = jnp.dot(
        one_hot, time_gain, precision=lax.Precision.HIGHEST, preferred_element_type=jnp.float32
    )
    skip_fwd = lax.dynamic_index_in_dim(skip_buffer[0], slot_ids[0], 0, False).astype(jnp.float32)
    skip_bwd = lax.dynamic_index_in_dim(skip_buffer[0], slot_ids[1], 0, False).astype(jnp.float32)
    saved = lax.dynamic_index_in_dim(stored_inputs[0], slot_ids[1], 0, False).astype(jnp.float32)

    saved_normed, saved_factor = normalize(saved)
    slope = silu_slope(saved_normed)
    cot_source, slope = lax.optimization_barrier((cot_carried[0], slope))
    returned = shifted(cot_source, "section", -1)

    normed, factor = normalize(x_in.astype(jnp.float32))
    acted = jax.nn.silu(normed).astype(jnp.bfloat16)
    stacked = jnp.concatenate([frame_shift(acted, k - 1) for k in range(3)], 0)
    partial = lax.dot_general(
        weight.reshape(3 * rows, -1),
        stacked,
        (((0,), (0,)), ((), ())),
        preferred_element_type=jnp.float32,
    ).reshape(2, 2, rows, -1)
    returned, partial = lax.optimization_barrier((returned, partial))
    mate_part = swap_core(pick(partial, 1 - core, 1))

    cot_in = jnp.where(section_place == sections - 1, reward_head, returned)
    cot_total = cot_in.astype(jnp.float32) + jnp.where(encoder, skip_bwd, jnp.zeros_like(skip_bwd))
    scaled = (cot_total * gains[1][:, None]).astype(jnp.bfloat16)
    scaled, mate_part = lax.optimization_barrier((scaled, mate_part))
    other = swap_chip(scaled)
    chip_sum = pick(partial, core, 1) + mate_part
    far = swap_chip(pick(chip_sum, 1 - chip, 0).astype(jnp.bfloat16))
    cot_source, chip_sum = lax.optimization_barrier((cot_source, chip_sum))
    mirrored_cot = lax.ppermute(
        cot_source, "section", [(sections - s, s) for s in range(1, sections // 2)]
    )
    far, other = lax.optimization_barrier((far, other))
    conv_out = pick(chip_sum, chip, 0) + far.astype(jnp.float32)
    added = jnp.where(encoder, jnp.zeros_like(skip_fwd), skip_fwd)
    act_out = (x_in.astype(jnp.float32) + conv_out * gains[0][:, None] + added).astype(jnp.bfloat16)
    mirrored_act = lax.ppermute(
        act_out, "section", [(s, sections - 1 - s) for s in range(sections // 2)]
    )

    pair = jnp.stack([jnp.where(chip == 0, scaled, other), jnp.where(chip == 0, other, scaled)])
    mate = swap_core(pair)
    mate, act_out = lax.optimization_barrier((mate, act_out))
    whole = jnp.stack([jnp.where(core == 0, pair, mate), jnp.where(core == 0, mate, pair)], 1)
    folded = jnp.einsum(
        "kio,or->kir",
        weight,
        whole.reshape(4 * rows, -1),
        preferred_element_type=jnp.float32,
    )
    d_acted = frame_shift(folded[0], 1) + folded[1] + frame_shift(folded[2], -1)
    d_normed = d_acted * slope
    cot_out = (cot_total + norm_back(saved_normed, saved_factor, d_normed)).astype(jnp.bfloat16)

    mirrored_cot, mirrored_act, cot_out = lax.optimization_barrier(
        (mirrored_cot, mirrored_act, cot_out)
    )
    mirrored_cot = jnp.where(section_place == 0, reward_head, mirrored_cot)
    mirror_in = jnp.where(encoder, mirrored_cot, mirrored_act)
    return (act_out[None], cot_out[None], mirror_in[None])


def solution(mesh):
    placed = (
        P("section", "ch", None),
        P("section", "ch", None),
        P("ch", None),
        P("ch", None),
        P("section", None, "ch", None),
        P("section", None, "ch", None),
        P("section", None, "ch", None),
        P(None, "ch"),
        P("section", None),
        P("section", None),
    )
    return jax.shard_map(
        local,
        mesh=mesh,
        in_specs=placed,
        out_specs=(P("section", "ch", None), P("section", "ch", None), P("section", "ch", None)),
        check_vma=False,
    )
```

```python
import jax
import jax.numpy as jnp
from jax import lax
from jax.experimental import pallas as pl
from jax.experimental.pallas import tpu as pltpu
from jax.sharding import PartitionSpec as P

C = 1280
GROUPS = 32
CELLS = 64
WIDTH = C // GROUPS

epsilon = 1e-05

VMEM = pl.BlockSpec(memory_space=pltpu.VMEM)
SMEM = pl.BlockSpec(memory_space=pltpu.SMEM)


def shifted(block, axis, distance):
    devices = range(lax.axis_size(axis))
    route = [(i - distance, i) for i in devices if i - distance in devices]
    return lax.ppermute(block, axis, route)


def swap_core(block):
    return lax.ppermute(block, "ch", [(0, 1), (1, 0), (2, 3), (3, 2)])


def swap_chip(block):
    return lax.ppermute(block, "ch", [(0, 2), (2, 0), (1, 3), (3, 1)])


def frame_shift(values, frames_by):
    step = frames_by * CELLS
    if step == 0:
        return values
    width = values.shape[1]
    lane = lax.broadcasted_iota(jnp.int32, values.shape, 1)
    rolled = pltpu.roll(values, (-step) % width, 1)
    kept = lane < width - step if step > 0 else lane >= -step
    return jnp.where(kept, rolled, 0.0)


def group_mean(grouped):
    total = jnp.sum(jnp.sum(grouped, axis=1, keepdims=True), axis=2, keepdims=True)
    return total * (1.0 / (grouped.shape[1] * grouped.shape[2]))


def by_group(values):
    return values.reshape(values.shape[0] // WIDTH, WIDTH, values.shape[1])


def normalize(values):
    grouped = by_group(values)
    centred = grouped - group_mean(grouped)
    factor = lax.rsqrt(group_mean(centred * centred) + epsilon)
    return (centred * factor).reshape(values.shape), factor


def column(table_ref, stamp):
    width = table_ref.shape[1]
    row = jnp.broadcast_to(table_ref[pl.ds(stamp, 1), :], (width, width))
    across = lax.broadcasted_iota(jnp.int32, (width, width), 0)
    along = lax.broadcasted_iota(jnp.int32, (width, width), 1)
    return jnp.sum(jnp.where(across == along, row, 0.0), axis=1, keepdims=True)


def transpose_kernel(weight_ref, out_ref):
    depth = weight_ref.shape[0]
    for start in range(0, depth, 128):
        size = min(128, depth - start)
        out_ref[:, start : start + size] = weight_ref[start : start + size, :].T


def forward_kernel(place_ref, arrived_ref, entry_ref, weight_ref, mate_ref, stacked_ref):
    rows = arrived_ref.shape[0]
    first = place_ref[0] == 0
    x_in = jnp.where(first, entry_ref[...], arrived_ref[...]).astype(jnp.float32)
    normed, _ = normalize(x_in)
    acted = normed / (1.0 + jnp.exp(-normed))
    for k in range(3):
        stacked_ref[k * rows : (k + 1) * rows, :] = frame_shift(acted, k - 1).astype(jnp.bfloat16)
    own_side(1 - place_ref[1], weight_ref, stacked_ref, mate_ref)


def own_side(core, weight_ref, stacked_ref, out_ref):
    rows = out_ref.shape[1]
    for chip in range(2):
        start = pl.multiple_of((chip * 2 + core) * rows, rows)
        out_ref[chip] = jnp.dot(
            weight_ref[pl.ds(start, rows), :], stacked_ref[...], preferred_element_type=jnp.float32
        )


def own_kernel(place_ref, weight_ref, stacked_ref, own_ref):
    own_side(place_ref[1], weight_ref, stacked_ref, own_ref)


def cotangent(place_ref, plan_ref, returned_ref, reward_ref, skip_ref):
    last = place_ref[3] == 1
    cot_in = jnp.where(last, reward_ref[...], returned_ref[...])
    skip = skip_ref[plan_ref[0, 1]].astype(jnp.float32)
    skip = jnp.where(place_ref[4] == 1, skip, 0.0)
    return cot_in, cot_in.astype(jnp.float32) + skip


def scaled_kernel(
    place_ref, plan_ref, stamps_ref, returned_ref, reward_ref, skip_ref, gain_ref, scaled_ref
):
    _, cot_total = cotangent(place_ref, plan_ref, returned_ref, reward_ref, skip_ref)
    scaled_ref[...] = (cot_total * column(gain_ref, stamps_ref[0, 1])).astype(jnp.bfloat16)


def halves_kernel(place_ref, own_ref, mate_ref, near_ref, far_ref):
    chip = place_ref[2]
    near_ref[...] = own_ref[chip] + mate_ref[chip]
    far_ref[...] = (own_ref[1 - chip] + mate_ref[1 - chip]).astype(jnp.bfloat16)


def output_kernel(
    place_ref,
    plan_ref,
    stamps_ref,
    near_ref,
    far_ref,
    arrived_ref,
    entry_ref,
    skip_ref,
    gain_ref,
    returned_ref,
    reward_ref,
    out_ref,
    sent_ref,
):
    x_in = jnp.where(place_ref[0] == 0, entry_ref[...], arrived_ref[...]).astype(jnp.float32)
    encoder = place_ref[4] == 1
    skip = jnp.where(encoder, 0.0, skip_ref[plan_ref[0, 0]].astype(jnp.float32))
    conv_sum = near_ref[...] + far_ref[...].astype(jnp.float32)
    act_out = (x_in + conv_sum * column(gain_ref, stamps_ref[0, 0]) + skip).astype(jnp.bfloat16)
    cot_in = jnp.where(place_ref[3] == 1, reward_ref[...], returned_ref[...])
    out_ref[...] = act_out
    sent_ref[...] = jnp.where(encoder, act_out, cot_in)


def pair_kernel(scaled_ref, other_ref, pair_ref):
    pair_ref[0] = scaled_ref[...]
    pair_ref[1] = other_ref[...]


def gradient_kernel(
    place_ref,
    plan_ref,
    stored_ref,
    returned_ref,
    reward_ref,
    skip_ref,
    scaled_ref,
    other_ref,
    mate_ref,
    weight_ref,
    out_ref,
    whole_ref,
):
    rows = scaled_ref.shape[0]
    core, chip = place_ref[1], place_ref[2]

    def put(chip, core, block):
        whole_ref[pl.ds(pl.multiple_of((chip * 2 + core) * rows, rows), rows), :] = block

    put(chip, core, scaled_ref[...])
    put(1 - chip, core, other_ref[...])
    put(chip, 1 - core, mate_ref[0])
    put(1 - chip, 1 - core, mate_ref[1])
    _, cot_total = cotangent(place_ref, plan_ref, returned_ref, reward_ref, skip_ref)
    normed, factor = normalize(stored_ref[plan_ref[0, 1]].astype(jnp.float32))
    sigmoid = 1.0 / (1.0 + jnp.exp(-normed))
    slope = sigmoid * (1.0 + normed * (1.0 - sigmoid))
    folded = jnp.dot(weight_ref[...], whole_ref[...], preferred_element_type=jnp.float32)
    d_acted = (
        frame_shift(folded[:rows], 1)
        + folded[rows : 2 * rows]
        + frame_shift(folded[2 * rows :], -1)
    )
    d_normed = by_group(d_acted * slope)
    grouped = by_group(normed)
    result = factor * (
        d_normed - group_mean(d_normed) - grouped * group_mean(d_normed * grouped)
    )
    out_ref[...] = (cot_total + result.reshape(cot_total.shape)).astype(jnp.bfloat16)


def call(kernel, outs, specs, args, scratch=(), cost=0.0, limit=16):
    return pl.pallas_call(
        kernel,
        out_shape=[jax.ShapeDtypeStruct(shape, kind) for shape, kind in outs],
        in_specs=specs,
        out_specs=[VMEM] * len(outs),
        scratch_shapes=list(scratch),
        compiler_params=pltpu.CompilerParams(vmem_limit_bytes=limit * 2**20),
        cost_estimate=pl.CostEstimate(
            flops=int(cost * 1e9), bytes_accessed=int(cost * 1e6), transcendentals=0
        ),
        name=kernel.__name__,
    )(*args)


def local(
    act_carried,
    cot_carried,
    entry_latent,
    reward_head,
    stored_inputs,
    skip_buffer,
    conv_weight,
    time_gain,
    plan,
    timesteps,
):
    sections = lax.axis_size("section")
    section = lax.axis_index("section")
    ch = lax.axis_index("ch")
    rows, cells = act_carried.shape[1:]
    weight = conv_weight[0].reshape(3 * rows, -1)
    full = weight.shape[1]
    stored, skips = stored_inputs[0], skip_buffer[0]
    last = (section == sections - 1).astype(jnp.int32)
    encoder = (section < sections // 2).astype(jnp.int32)
    place = jnp.stack([section, ch % 2, ch // 2, last, encoder])
    field = ((rows, cells), jnp.bfloat16)
    pair = ((2, rows, cells), jnp.float32)

    arrived = shifted(act_carried[0], "section", 1)
    returned = shifted(cot_carried[0], "section", -1)
    (turned,) = call(transpose_kernel, [((full, 3 * rows), jnp.bfloat16)], [VMEM], [weight])

    mate_side, stacked = call(
        forward_kernel,
        [pair, ((3 * rows, cells), jnp.bfloat16)],
        [SMEM, VMEM, VMEM, VMEM],
        [place, arrived, entry_latent, turned],
    )
    returned, mate_side = lax.optimization_barrier((returned, mate_side))
    mate_part = swap_core(mate_side)
    (own,) = call(own_kernel, [pair], [SMEM, VMEM, VMEM], [place, turned, stacked])
    returned, own = lax.optimization_barrier((returned, own))
    (scaled,) = call(
        scaled_kernel,
        [field],
        [SMEM] * 3 + [VMEM] * 4,
        [place, plan, timesteps, returned, reward_head, skips, time_gain],
    )
    scaled, mate_part = lax.optimization_barrier((scaled, mate_part))
    other = swap_chip(scaled)
    near, far_side = call(
        halves_kernel,
        [((rows, cells), jnp.float32), field],
        [SMEM, VMEM, VMEM],
        [place, own, mate_part],
    )
    far = swap_chip(far_side)
    (gathered,) = call(
        pair_kernel,
        [((2, rows, cells), jnp.bfloat16)],
        [VMEM, VMEM],
        [scaled, other],
        cost=10.0,
    )
    far, gathered = lax.optimization_barrier((far, gathered))
    mate = swap_core(gathered)
    act_out, sent = call(
        output_kernel,
        [field, field],
        [SMEM] * 3 + [VMEM] * 8,
        [
            place,
            plan,
            timesteps,
            near,
            far,
            arrived,
            entry_latent,
            skips,
            time_gain,
            returned,
            reward_head,
        ],
    )
    mirror_in = lax.ppermute(sent, "section", [(s, sections - 1 - s) for s in range(sections)])

    mate, act_out = lax.optimization_barrier((mate, act_out))
    (cot_out,) = call(
        gradient_kernel,
        [field],
        [SMEM] * 2 + [VMEM] * 8,
        [place, plan, stored, returned, reward_head, skips, scaled, other, mate, weight],
        scratch=[pltpu.VMEM((full, cells), jnp.bfloat16)],
        cost=30.0,
    )
    mirror_in, cot_out = lax.optimization_barrier((mirror_in, cot_out))
    return (act_out[None], cot_out[None], mirror_in[None])


def solution(mesh):
    placed = (
        P("section", "ch", None),
        P("section", "ch", None),
        P("ch", None),
        P("ch", None),
        P("section", None, "ch", None),
        P("section", None, "ch", None),
        P("section", None, "ch", None),
        P(None, "ch"),
        P("section", None),
        P("section", None),
    )
    return jax.shard_map(
        local,
        mesh=mesh,
        in_specs=placed,
        out_specs=(P("section", "ch", None), P("section", "ch", None), P("section", "ch", None)),
        check_vma=False,
    )
```

```python
import jax
import jax.numpy as jnp
from jax import lax
from jax.experimental import pallas as pl
from jax.experimental.pallas import tpu as pltpu
from jax.sharding import PartitionSpec as P

C = 1280
GROUPS = 32
CELLS = 64
WIDTH = C // GROUPS

epsilon = 1e-05

VMEM = pl.BlockSpec(memory_space=pltpu.VMEM)
SMEM = pl.BlockSpec(memory_space=pltpu.SMEM)


def shifted(block, axis, distance):
    devices = range(lax.axis_size(axis))
    route = [(i - distance, i) for i in devices if i - distance in devices]
    return lax.ppermute(block, axis, route)


def swap_core(block):
    return lax.ppermute(block, "ch", [(0, 1), (1, 0), (2, 3), (3, 2)])


def swap_chip(block):
    return lax.ppermute(block, "ch", [(0, 2), (2, 0), (1, 3), (3, 1)])


def frame_shift(values, frames_by):
    step = frames_by * CELLS
    if step == 0:
        return values
    width = values.shape[1]
    lane = lax.broadcasted_iota(jnp.int32, values.shape, 1)
    rolled = pltpu.roll(values, (-step) % width, 1)
    kept = lane < width - step if step > 0 else lane >= -step
    return jnp.where(kept, rolled, 0.0)


def group_mean(grouped):
    total = jnp.sum(jnp.sum(grouped, axis=1, keepdims=True), axis=2, keepdims=True)
    return total * (1.0 / (grouped.shape[1] * grouped.shape[2]))


def by_group(values):
    return values.reshape(values.shape[0] // WIDTH, WIDTH, values.shape[1])


def normalize(values):
    grouped = by_group(values)
    centred = grouped - group_mean(grouped)
    factor = lax.rsqrt(group_mean(centred * centred) + epsilon)
    return (centred * factor).reshape(values.shape), factor


def column(table_ref, stamp):
    width = table_ref.shape[1]
    row = jnp.broadcast_to(table_ref[pl.ds(stamp, 1), :], (width, width))
    across = lax.broadcasted_iota(jnp.int32, (width, width), 0)
    along = lax.broadcasted_iota(jnp.int32, (width, width), 1)
    return jnp.sum(jnp.where(across == along, row, 0.0), axis=1, keepdims=True)


def transpose_kernel(weight_ref, out_ref):
    depth = weight_ref.shape[0]
    for start in range(0, depth, 128):
        size = min(128, depth - start)
        out_ref[:, start : start + size] = weight_ref[start : start + size, :].T


def forward_kernel(place_ref, arrived_ref, entry_ref, weight_ref, mate_ref, stacked_ref):
    rows = arrived_ref.shape[0]
    first = place_ref[0] == 0
    x_in = jnp.where(first, entry_ref[...], arrived_ref[...]).astype(jnp.float32)
    normed, _ = normalize(x_in)
    acted = normed / (1.0 + jnp.exp(-normed))
    for k in range(3):
        stacked_ref[k * rows : (k + 1) * rows, :] = frame_shift(acted, k - 1).astype(jnp.bfloat16)
    own_side(1 - place_ref[1], weight_ref, stacked_ref, mate_ref)


def own_side(core, weight_ref, stacked_ref, out_ref):
    rows = out_ref.shape[1]
    for chip in range(2):
        start = pl.multiple_of((chip * 2 + core) * rows, rows)
        out_ref[chip] = jnp.dot(
            weight_ref[pl.ds(start, rows), :], stacked_ref[...], preferred_element_type=jnp.float32
        )


def own_kernel(place_ref, weight_ref, stacked_ref, own_ref):
    own_side(place_ref[1], weight_ref, stacked_ref, own_ref)


def cotangent(place_ref, plan_ref, returned_ref, reward_ref, skip_ref):
    last = place_ref[3] == 1
    cot_in = jnp.where(last, reward_ref[...], returned_ref[...])
    skip = skip_ref[plan_ref[0, 1]].astype(jnp.float32)
    skip = jnp.where(place_ref[4] == 1, skip, 0.0)
    return cot_in, cot_in.astype(jnp.float32) + skip


def scaled_kernel(
    place_ref, plan_ref, stamps_ref, returned_ref, reward_ref, skip_ref, gain_ref, scaled_ref
):
    _, cot_total = cotangent(place_ref, plan_ref, returned_ref, reward_ref, skip_ref)
    scaled_ref[...] = (cot_total * column(gain_ref, stamps_ref[0, 1])).astype(jnp.bfloat16)


def halves_kernel(place_ref, own_ref, mate_ref, near_ref, far_ref):
    chip = place_ref[2]
    near_ref[...] = own_ref[chip] + mate_ref[chip]
    far_ref[...] = (own_ref[1 - chip] + mate_ref[1 - chip]).astype(jnp.bfloat16)


def output_kernel(
    place_ref,
    plan_ref,
    stamps_ref,
    near_ref,
    far_ref,
    arrived_ref,
    entry_ref,
    skip_ref,
    gain_ref,
    out_ref,
):
    x_in = jnp.where(place_ref[0] == 0, entry_ref[...], arrived_ref[...]).astype(jnp.float32)
    skip = jnp.where(place_ref[4] == 1, 0.0, skip_ref[plan_ref[0, 0]].astype(jnp.float32))
    conv_sum = near_ref[...] + far_ref[...].astype(jnp.float32)
    act_out = (x_in + conv_sum * column(gain_ref, stamps_ref[0, 0]) + skip).astype(jnp.bfloat16)
    out_ref[...] = act_out


def choose_kernel(place_ref, cot_ref, act_ref, reward_ref, out_ref):
    cot = jnp.where(place_ref[0] == 0, reward_ref[...], cot_ref[...])
    out_ref[...] = jnp.where(place_ref[4] == 1, cot, act_ref[...])


def saved_kernel(plan_ref, stored_ref, normed_ref, factor_ref):
    normed, factor = normalize(stored_ref[plan_ref[0, 1]].astype(jnp.float32))
    normed_ref[...] = normed
    factor_ref[...] = jnp.broadcast_to(factor, factor_ref.shape)


def gradient_kernel(
    place_ref,
    plan_ref,
    normed_ref,
    factor_ref,
    returned_ref,
    reward_ref,
    skip_ref,
    scaled_ref,
    other_ref,
    mate_ref,
    mate_low_ref,
    mate_high_ref,
    weight_ref,
    out_ref,
    whole_ref,
):
    rows = scaled_ref.shape[0]
    core, chip = place_ref[1], place_ref[2]

    def put(chip, core, block, skipped=0):
        start = pl.multiple_of((chip * 2 + core) * rows + skipped, 32)
        whole_ref[pl.ds(start, block.shape[0]), :] = block

    put(chip, core, scaled_ref[...])
    put(1 - chip, core, other_ref[...])
    put(chip, 1 - core, mate_ref[...])
    put(1 - chip, 1 - core, mate_low_ref[...])
    put(1 - chip, 1 - core, mate_high_ref[...], rows // 2)
    _, cot_total = cotangent(place_ref, plan_ref, returned_ref, reward_ref, skip_ref)
    normed = normed_ref[...]
    sigmoid = 1.0 / (1.0 + jnp.exp(-normed))
    slope = sigmoid * (1.0 + normed * (1.0 - sigmoid))
    folded = jnp.dot(weight_ref[...], whole_ref[...], preferred_element_type=jnp.float32)
    d_acted = (
        frame_shift(folded[:rows], 1)
        + folded[rows : 2 * rows]
        + frame_shift(folded[2 * rows :], -1)
    )
    d_normed = by_group(d_acted * slope)
    grouped = by_group(normed)
    result = factor_ref[:, :1, :1] * (
        d_normed - group_mean(d_normed) - grouped * group_mean(d_normed * grouped)
    )
    out_ref[...] = (cot_total + result.reshape(cot_total.shape)).astype(jnp.bfloat16)


def call(kernel, outs, specs, args, scratch=(), cost=0.0, limit=16):
    return pl.pallas_call(
        kernel,
        out_shape=[jax.ShapeDtypeStruct(shape, kind) for shape, kind in outs],
        in_specs=specs,
        out_specs=[VMEM] * len(outs),
        scratch_shapes=list(scratch),
        compiler_params=pltpu.CompilerParams(vmem_limit_bytes=limit * 2**20),
        cost_estimate=pl.CostEstimate(
            flops=int(cost * 1e9), bytes_accessed=int(cost * 1e6), transcendentals=0
        ),
        name=kernel.__name__,
    )(*args)


def local(
    act_carried,
    cot_carried,
    entry_latent,
    reward_head,
    stored_inputs,
    skip_buffer,
    conv_weight,
    time_gain,
    plan,
    timesteps,
):
    sections = lax.axis_size("section")
    section = lax.axis_index("section")
    ch = lax.axis_index("ch")
    rows, cells = act_carried.shape[1:]
    weight = conv_weight[0].reshape(3 * rows, -1)
    full = weight.shape[1]
    stored, skips = stored_inputs[0], skip_buffer[0]
    last = (section == sections - 1).astype(jnp.int32)
    encoder = (section < sections // 2).astype(jnp.int32)
    place = jnp.stack([section, ch % 2, ch // 2, last, encoder])
    field = ((rows, cells), jnp.bfloat16)
    pair = ((2, rows, cells), jnp.float32)

    arrived = shifted(act_carried[0], "section", 1)
    (turned,) = call(transpose_kernel, [((full, 3 * rows), jnp.bfloat16)], [VMEM], [weight], cost=20.0)
    cotangents, turned = lax.optimization_barrier((cot_carried[0], turned))
    mirrored_cot = lax.ppermute(
        cotangents, "section", [(sections - s, s) for s in range(1, sections // 2)]
    )

    mate_side, stacked = call(
        forward_kernel,
        [pair, ((3 * rows, cells), jnp.bfloat16)],
        [SMEM, VMEM, VMEM, VMEM],
        [place, arrived, entry_latent, turned],
    )
    mate_part = swap_core(mate_side)
    cotangents, mate_side = lax.optimization_barrier((cotangents, mate_side))
    returned = shifted(cotangents, "section", -1)
    (own,) = call(own_kernel, [pair], [SMEM, VMEM, VMEM], [place, turned, stacked], cost=20.0)
    near, far_side = call(
        halves_kernel,
        [((rows, cells), jnp.float32), field],
        [SMEM, VMEM, VMEM],
        [place, own, mate_part],
    )
    far = swap_chip(far_side)
    returned, far_side = lax.optimization_barrier((returned, far_side))
    (scaled,) = call(
        scaled_kernel,
        [field],
        [SMEM] * 3 + [VMEM] * 4,
        [place, plan, timesteps, returned, reward_head, skips, time_gain],
    )
    other = swap_chip(scaled)
    stored, far_side = lax.optimization_barrier((stored, far_side))
    saved_normed, saved_factor = call(
        saved_kernel,
        [((rows, cells), jnp.float32), ((rows // WIDTH, 8, 128), jnp.float32)],
        [SMEM, VMEM],
        [plan, stored],
        cost=20.0,
    )
    far, scaled, saved_normed = lax.optimization_barrier((far, scaled, saved_normed))
    (act_out,) = call(
        output_kernel,
        [field],
        [SMEM] * 3 + [VMEM] * 6,
        [place, plan, timesteps, near, far, arrived, entry_latent, skips, time_gain],
    )
    mirrored_act = lax.ppermute(
        act_out, "section", [(s, sections - 1 - s) for s in range(sections // 2)]
    )

    other, scaled, act_out = lax.optimization_barrier((other, scaled, act_out))
    half = rows // 2
    mates = [swap_core(part) for part in (scaled, other[:half], other[half:])]
    (cot_out,) = call(
        gradient_kernel,
        [field],
        [SMEM] * 2 + [VMEM] * 11,
        [place, plan, saved_normed, saved_factor, returned, reward_head, skips, scaled, other, *mates, weight],
        scratch=[pltpu.VMEM((full, cells), jnp.bfloat16)],
    )
    mirrored_cot, mirrored_act, cot_out = lax.optimization_barrier(
        (mirrored_cot, mirrored_act, cot_out)
    )
    (mirror_in,) = call(
        choose_kernel,
        [field],
        [SMEM] + [VMEM] * 3,
        [place, mirrored_cot, mirrored_act, reward_head],
    )
    return (act_out[None], cot_out[None], mirror_in[None])


def solution(mesh):
    placed = (
        P("section", "ch", None),
        P("section", "ch", None),
        P("ch", None),
        P("ch", None),
        P("section", None, "ch", None),
        P("section", None, "ch", None),
        P("section", None, "ch", None),
        P(None, "ch"),
        P("section", None),
        P("section", None),
    )
    return jax.shard_map(
        local,
        mesh=mesh,
        in_specs=placed,
        out_specs=(P("section", "ch", None), P("section", "ch", None), P("section", "ch", None)),
        check_vma=False,
    )
```

```python
import jax
import jax.numpy as jnp
from jax import lax
from jax.experimental import pallas as pl
from jax.experimental.pallas import tpu as pltpu
from jax.sharding import PartitionSpec as P

C = 1280
GROUPS = 32
CELLS = 64
WIDTH = C // GROUPS

epsilon = 1e-05

VMEM = pl.BlockSpec(memory_space=pltpu.VMEM)
SMEM = pl.BlockSpec(memory_space=pltpu.SMEM)


def shifted(block, axis, distance):
    devices = range(lax.axis_size(axis))
    route = [(i - distance, i) for i in devices if i - distance in devices]
    return lax.ppermute(block, axis, route)


def swap_core(block):
    return lax.ppermute(block, "ch", [(0, 1), (1, 0), (2, 3), (3, 2)])


def swap_chip(block):
    return lax.ppermute(block, "ch", [(0, 2), (2, 0), (1, 3), (3, 1)])


def frame_shift(values, frames_by):
    step = frames_by * CELLS
    if step == 0:
        return values
    width = values.shape[1]
    lane = lax.broadcasted_iota(jnp.int32, values.shape, 1)
    rolled = pltpu.roll(values, (-step) % width, 1)
    kept = lane < width - step if step > 0 else lane >= -step
    return jnp.where(kept, rolled, 0.0)


def group_mean(grouped):
    total = jnp.sum(jnp.sum(grouped, axis=1, keepdims=True), axis=2, keepdims=True)
    return total * (1.0 / (grouped.shape[1] * grouped.shape[2]))


def by_group(values):
    return values.reshape(values.shape[0] // WIDTH, WIDTH, values.shape[1])


def normalize(values):
    grouped = by_group(values)
    centred = grouped - group_mean(grouped)
    factor = lax.rsqrt(group_mean(centred * centred) + epsilon)
    return (centred * factor).reshape(values.shape), factor


def column(table_ref, stamp):
    width = table_ref.shape[1]
    row = jnp.broadcast_to(table_ref[pl.ds(stamp, 1), :], (width, width))
    across = lax.broadcasted_iota(jnp.int32, (width, width), 0)
    along = lax.broadcasted_iota(jnp.int32, (width, width), 1)
    return jnp.sum(jnp.where(across == along, row, 0.0), axis=1, keepdims=True)


def transpose_kernel(weight_ref, out_ref):
    depth = weight_ref.shape[0]
    for start in range(0, depth, 128):
        size = min(128, depth - start)
        out_ref[:, start : start + size] = weight_ref[start : start + size, :].T


def forward_kernel(place_ref, arrived_ref, entry_ref, weight_ref, mate_ref, stacked_ref):
    rows = arrived_ref.shape[0]
    first = place_ref[0] == 0
    x_in = jnp.where(first, entry_ref[...], arrived_ref[...]).astype(jnp.float32)
    normed, _ = normalize(x_in)
    acted = normed / (1.0 + jnp.exp(-normed))
    for k in range(3):
        stacked_ref[k * rows : (k + 1) * rows, :] = frame_shift(acted, k - 1).astype(jnp.bfloat16)
    own_side(1 - place_ref[1], weight_ref, stacked_ref, mate_ref)


def own_side(core, weight_ref, stacked_ref, out_ref):
    rows = out_ref.shape[1]
    for chip in range(2):
        start = pl.multiple_of((chip * 2 + core) * rows, rows)
        out_ref[chip] = jnp.dot(
            weight_ref[pl.ds(start, rows), :], stacked_ref[...], preferred_element_type=jnp.float32
        )


def own_kernel(place_ref, weight_ref, stacked_ref, own_ref):
    own_side(place_ref[1], weight_ref, stacked_ref, own_ref)


def prepare_kernel(
    place_ref, plan_ref, stamps_ref, skip_ref, gain_ref, columns_ref, added_ref, extra_ref
):
    for way in range(2):
        columns_ref[way] = jnp.broadcast_to(
            column(gain_ref, stamps_ref[0, way]), columns_ref.shape[1:]
        )
    encoder = place_ref[4] == 1
    added = skip_ref[plan_ref[0, 0]]
    extra = skip_ref[plan_ref[0, 1]]
    added_ref[...] = jnp.where(encoder, jnp.zeros_like(added), added)
    extra_ref[...] = jnp.where(encoder, extra, jnp.zeros_like(extra))


def cotangent(place_ref, returned_ref, reward_ref, extra_ref):
    cot_in = jnp.where(place_ref[3] == 1, reward_ref[...], returned_ref[...])
    return cot_in.astype(jnp.float32) + extra_ref[...].astype(jnp.float32)


def scaled_kernel(place_ref, returned_ref, reward_ref, extra_ref, columns_ref, scaled_ref):
    cot_total = cotangent(place_ref, returned_ref, reward_ref, extra_ref)
    scaled_ref[...] = (cot_total * columns_ref[1][:, :1]).astype(jnp.bfloat16)


def halves_kernel(place_ref, own_ref, mate_ref, near_ref, far_ref):
    chip = place_ref[2]
    near_ref[...] = own_ref[chip] + mate_ref[chip]
    far_ref[...] = (own_ref[1 - chip] + mate_ref[1 - chip]).astype(jnp.bfloat16)


def output_kernel(
    place_ref, near_ref, far_ref, arrived_ref, entry_ref, added_ref, columns_ref, out_ref
):
    x_in = jnp.where(place_ref[0] == 0, entry_ref[...], arrived_ref[...]).astype(jnp.float32)
    conv_sum = near_ref[...] + far_ref[...].astype(jnp.float32)
    act_out = x_in + conv_sum * columns_ref[0][:, :1] + added_ref[...].astype(jnp.float32)
    out_ref[...] = act_out.astype(jnp.bfloat16)


def choose_kernel(place_ref, cot_ref, act_ref, reward_ref, out_ref, sem):
    def put(chosen_ref):
        copy = pltpu.make_async_copy(chosen_ref, out_ref, sem)
        copy.start()
        copy.wait()

    @pl.when(place_ref[0] == 0)
    def _():
        put(reward_ref)

    @pl.when((place_ref[4] == 1) & (place_ref[0] != 0))
    def _():
        put(cot_ref)

    @pl.when(place_ref[4] == 0)
    def _():
        put(act_ref)


def saved_kernel(plan_ref, stored_ref, normed_ref, factor_ref):
    normed, factor = normalize(stored_ref[plan_ref[0, 1]].astype(jnp.float32))
    normed_ref[...] = normed
    factor_ref[...] = jnp.broadcast_to(factor, factor_ref.shape)


def gradient_kernel(
    place_ref,
    normed_ref,
    factor_ref,
    returned_ref,
    reward_ref,
    extra_ref,
    scaled_ref,
    other_ref,
    mate_ref,
    mate_low_ref,
    mate_high_ref,
    weight_ref,
    out_ref,
    whole_ref,
):
    rows = scaled_ref.shape[0]
    core, chip = place_ref[1], place_ref[2]

    def put(chip, core, block, skipped=0):
        start = pl.multiple_of((chip * 2 + core) * rows + skipped, 32)
        whole_ref[pl.ds(start, block.shape[0]), :] = block

    put(chip, core, scaled_ref[...])
    put(1 - chip, core, other_ref[...])
    put(chip, 1 - core, mate_ref[...])
    put(1 - chip, 1 - core, mate_low_ref[...])
    put(1 - chip, 1 - core, mate_high_ref[...], rows // 2)
    cot_total = cotangent(place_ref, returned_ref, reward_ref, extra_ref)
    normed = normed_ref[...]
    sigmoid = 1.0 / (1.0 + jnp.exp(-normed))
    slope = sigmoid * (1.0 + normed * (1.0 - sigmoid))
    folded = jnp.dot(weight_ref[...], whole_ref[...], preferred_element_type=jnp.float32)
    d_acted = (
        frame_shift(folded[:rows], 1)
        + folded[rows : 2 * rows]
        + frame_shift(folded[2 * rows :], -1)
    )
    d_normed = by_group(d_acted * slope)
    grouped = by_group(normed)
    result = factor_ref[:, :1, :1] * (
        d_normed - group_mean(d_normed) - grouped * group_mean(d_normed * grouped)
    )
    out_ref[...] = (cot_total + result.reshape(cot_total.shape)).astype(jnp.bfloat16)


def call(kernel, outs, specs, args, scratch=(), cost=0.0, limit=16, where=VMEM):
    return pl.pallas_call(
        kernel,
        out_shape=[jax.ShapeDtypeStruct(shape, kind) for shape, kind in outs],
        in_specs=specs,
        out_specs=[where] * len(outs),
        scratch_shapes=list(scratch),
        compiler_params=pltpu.CompilerParams(vmem_limit_bytes=limit * 2**20),
        cost_estimate=pl.CostEstimate(
            flops=int(cost * 1e9), bytes_accessed=int(cost * 1e6), transcendentals=0
        ),
        name=kernel.__name__,
    )(*args)


def local(
    act_carried,
    cot_carried,
    entry_latent,
    reward_head,
    stored_inputs,
    skip_buffer,
    conv_weight,
    time_gain,
    plan,
    timesteps,
):
    sections = lax.axis_size("section")
    section = lax.axis_index("section")
    ch = lax.axis_index("ch")
    rows, cells = act_carried.shape[1:]
    weight = conv_weight[0].reshape(3 * rows, -1)
    full = weight.shape[1]
    stored, skips = stored_inputs[0], skip_buffer[0]
    last = (section == sections - 1).astype(jnp.int32)
    encoder = (section < sections // 2).astype(jnp.int32)
    place = jnp.stack([section, ch % 2, ch // 2, last, encoder])
    field = ((rows, cells), jnp.bfloat16)
    pair = ((2, rows, cells), jnp.float32)

    arrived = shifted(act_carried[0], "section", 1)
    (turned,) = call(transpose_kernel, [((full, 3 * rows), jnp.bfloat16)], [VMEM], [weight], cost=20.0)
    turned, skips, time_gain = lax.optimization_barrier((turned, skips, time_gain))
    gains, added, extra = call(
        prepare_kernel,
        [((2, rows, 128), jnp.float32), field, field],
        [SMEM] * 3 + [VMEM] * 2,
        [place, plan, timesteps, skips, time_gain],
        cost=20.0,
    )
    cotangents, gains, turned = lax.optimization_barrier((cot_carried[0], gains, turned))
    mirrored_cot = lax.ppermute(
        cotangents, "section", [(sections - s, s) for s in range(1, sections // 2)]
    )

    mate_side, stacked = call(
        forward_kernel,
        [pair, ((3 * rows, cells), jnp.bfloat16)],
        [SMEM, VMEM, VMEM, VMEM],
        [place, arrived, entry_latent, turned],
    )
    mate_part = swap_core(mate_side)
    cotangents, mate_side = lax.optimization_barrier((cotangents, mate_side))
    returned = shifted(cotangents, "section", -1)
    (own,) = call(own_kernel, [pair], [SMEM, VMEM, VMEM], [place, turned, stacked], cost=20.0)
    near, far_side = call(
        halves_kernel,
        [((rows, cells), jnp.float32), field],
        [SMEM, VMEM, VMEM],
        [place, own, mate_part],
    )
    far = swap_chip(far_side)
    returned, far_side = lax.optimization_barrier((returned, far_side))
    (scaled,) = call(
        scaled_kernel,
        [field],
        [SMEM] + [VMEM] * 4,
        [place, returned, reward_head, extra, gains],
    )
    other = swap_chip(scaled)
    stored, far_side = lax.optimization_barrier((stored, far_side))
    saved_normed, saved_factor = call(
        saved_kernel,
        [((rows, cells), jnp.float32), ((rows // WIDTH, 8, 128), jnp.float32)],
        [SMEM, VMEM],
        [plan, stored],
        cost=20.0,
    )
    far, scaled, saved_normed = lax.optimization_barrier((far, scaled, saved_normed))
    (act_out,) = call(
        output_kernel,
        [field],
        [SMEM] + [VMEM] * 6,
        [place, near, far, arrived, entry_latent, added, gains],
    )
    mirrored_act = lax.ppermute(
        act_out, "section", [(s, sections - 1 - s) for s in range(sections // 2)]
    )

    other, scaled, act_out = lax.optimization_barrier((other, scaled, act_out))
    half = rows // 2
    mates = [swap_core(part) for part in (scaled, other[:half], other[half:])]
    (cot_out,) = call(
        gradient_kernel,
        [field],
        [SMEM] + [VMEM] * 11,
        [
            place,
            saved_normed,
            saved_factor,
            returned,
            reward_head,
            extra,
            scaled,
            other,
            *mates,
            weight,
        ],
        scratch=[pltpu.VMEM((full, cells), jnp.bfloat16)],
    )
    mirrored_cot, mirrored_act, cot_out = lax.optimization_barrier(
        (mirrored_cot, mirrored_act, cot_out)
    )
    (mirror_in,) = call(
        choose_kernel,
        [field],
        [SMEM] + [VMEM] * 3,
        [place, mirrored_cot, mirrored_act, reward_head],
        scratch=[pltpu.SemaphoreType.DMA],
        where=pl.BlockSpec(memory_space=pl.ANY),
    )
    return (act_out[None], cot_out[None], mirror_in[None])


def solution(mesh):
    placed = (
        P("section", "ch", None),
        P("section", "ch", None),
        P("ch", None),
        P("ch", None),
        P("section", None, "ch", None),
        P("section", None, "ch", None),
        P("section", None, "ch", None),
        P(None, "ch"),
        P("section", None),
        P("section", None),
    )
    return jax.shard_map(
        local,
        mesh=mesh,
        in_specs=placed,
        out_specs=(P("section", "ch", None), P("section", "ch", None), P("section", "ch", None)),
        check_vma=False,
    )
```

```python
import jax
import jax.numpy as jnp
from jax import lax
from jax.experimental import pallas as pl
from jax.experimental.pallas import tpu as pltpu
from jax.sharding import PartitionSpec as P

C = 1280
GROUPS = 32
CELLS = 64
WIDTH = C // GROUPS

epsilon = 1e-05

VMEM = pl.BlockSpec(memory_space=pltpu.VMEM)
SMEM = pl.BlockSpec(memory_space=pltpu.SMEM)


def shifted(block, axis, distance):
    devices = range(lax.axis_size(axis))
    route = [(i - distance, i) for i in devices if i - distance in devices]
    return lax.ppermute(block, axis, route)


def swap_core(block):
    return lax.ppermute(block, "ch", [(0, 1), (1, 0), (2, 3), (3, 2)])


def swap_chip(block):
    return lax.ppermute(block, "ch", [(0, 2), (2, 0), (1, 3), (3, 1)])


def frame_shift(values, frames_by):
    step = frames_by * CELLS
    if step == 0:
        return values
    width = values.shape[1]
    lane = lax.broadcasted_iota(jnp.int32, values.shape, 1)
    rolled = pltpu.roll(values, (-step) % width, 1)
    kept = lane < width - step if step > 0 else lane >= -step
    return jnp.where(kept, rolled, 0.0)


def group_mean(grouped):
    total = jnp.sum(jnp.sum(grouped, axis=1, keepdims=True), axis=2, keepdims=True)
    return total * (1.0 / (grouped.shape[1] * grouped.shape[2]))


def by_group(values):
    return values.reshape(values.shape[0] // WIDTH, WIDTH, values.shape[1])


def normalize(values):
    grouped = by_group(values)
    centred = grouped - group_mean(grouped)
    factor = lax.rsqrt(group_mean(centred * centred) + epsilon)
    return (centred * factor).reshape(values.shape), factor


def column(table_ref, stamp):
    width = table_ref.shape[1]
    row = jnp.broadcast_to(table_ref[pl.ds(stamp, 1), :], (width, width))
    across = lax.broadcasted_iota(jnp.int32, (width, width), 0)
    along = lax.broadcasted_iota(jnp.int32, (width, width), 1)
    return jnp.sum(jnp.where(across == along, row, 0.0), axis=1, keepdims=True)


def transpose_kernel(weight_ref, out_ref):
    depth = weight_ref.shape[0]
    for start in range(0, depth, 128):
        size = min(128, depth - start)
        out_ref[:, start : start + size] = weight_ref[start : start + size, :].T


def forward_kernel(place_ref, arrived_ref, entry_ref, weight_ref, mate_ref, stacked_ref):
    rows = arrived_ref.shape[0]
    first = place_ref[0] == 0
    x_in = jnp.where(first, entry_ref[...], arrived_ref[...]).astype(jnp.float32)
    normed, _ = normalize(x_in)
    acted = normed / (1.0 + jnp.exp(-normed))
    for k in range(3):
        stacked_ref[k * rows : (k + 1) * rows, :] = frame_shift(acted, k - 1).astype(jnp.bfloat16)
    own_side(1 - place_ref[1], weight_ref, stacked_ref, mate_ref)


def own_side(core, weight_ref, stacked_ref, out_ref):
    rows = out_ref.shape[1]
    for chip in range(2):
        start = pl.multiple_of((chip * 2 + core) * rows, rows)
        out_ref[chip] = jnp.dot(
            weight_ref[pl.ds(start, rows), :], stacked_ref[...], preferred_element_type=jnp.float32
        )


def own_kernel(place_ref, weight_ref, stacked_ref, own_ref):
    own_side(place_ref[1], weight_ref, stacked_ref, own_ref)


def prepare_kernel(
    place_ref, plan_ref, stamps_ref, skip_ref, gain_ref, columns_ref, added_ref, extra_ref
):
    for way in range(2):
        columns_ref[way] = jnp.broadcast_to(
            column(gain_ref, stamps_ref[0, way]), columns_ref.shape[1:]
        )
    encoder = place_ref[4] == 1
    added = skip_ref[plan_ref[0, 0]]
    extra = skip_ref[plan_ref[0, 1]]
    added_ref[...] = jnp.where(encoder, jnp.zeros_like(added), added)
    extra_ref[...] = jnp.where(encoder, extra, jnp.zeros_like(extra))


def cotangent(place_ref, returned_ref, reward_ref, extra_ref):
    cot_in = jnp.where(place_ref[3] == 1, reward_ref[...], returned_ref[...])
    return cot_in.astype(jnp.float32) + extra_ref[...].astype(jnp.float32)


def scaled_kernel(place_ref, returned_ref, reward_ref, extra_ref, columns_ref, scaled_ref):
    cot_total = cotangent(place_ref, returned_ref, reward_ref, extra_ref)
    scaled_ref[...] = (cot_total * columns_ref[1][:, :1]).astype(jnp.bfloat16)


def halves_kernel(place_ref, own_ref, mate_ref, near_ref, far_ref):
    chip = place_ref[2]
    near_ref[...] = own_ref[chip] + mate_ref[chip]
    far_ref[...] = (own_ref[1 - chip] + mate_ref[1 - chip]).astype(jnp.bfloat16)


def output_kernel(
    place_ref,
    near_ref,
    far_ref,
    arrived_ref,
    entry_ref,
    added_ref,
    columns_ref,
    returned_ref,
    reward_ref,
    out_ref,
    sent_ref,
):
    x_in = jnp.where(place_ref[0] == 0, entry_ref[...], arrived_ref[...]).astype(jnp.float32)
    conv_sum = near_ref[...] + far_ref[...].astype(jnp.float32)
    act_out = x_in + conv_sum * columns_ref[0][:, :1] + added_ref[...].astype(jnp.float32)
    act_out = act_out.astype(jnp.bfloat16)
    out_ref[...] = act_out
    cot_in = jnp.where(place_ref[3] == 1, reward_ref[...], returned_ref[...])
    sent_ref[...] = jnp.where(place_ref[4] == 1, act_out, cot_in)


def saved_kernel(plan_ref, stored_ref, normed_ref, factor_ref):
    normed, factor = normalize(stored_ref[plan_ref[0, 1]].astype(jnp.float32))
    normed_ref[...] = normed
    factor_ref[...] = jnp.broadcast_to(factor, factor_ref.shape)


def split_kernel(scaled_ref, other_ref, *part_refs):
    half = part_refs[0].shape[0]
    for i, part_ref in enumerate(part_refs):
        source_ref = (scaled_ref, other_ref)[i // 2]
        part_ref[...] = source_ref[i % 2 * half : (i % 2 + 1) * half, :]


def gradient_kernel(
    place_ref,
    normed_ref,
    factor_ref,
    returned_ref,
    reward_ref,
    extra_ref,
    scaled_ref,
    other_ref,
    mate_low_ref,
    mate_high_ref,
    other_low_ref,
    other_high_ref,
    weight_ref,
    out_ref,
    whole_ref,
):
    rows = scaled_ref.shape[0]
    core, chip = place_ref[1], place_ref[2]

    def put(chip, core, block, skipped=0):
        start = pl.multiple_of((chip * 2 + core) * rows + skipped, 32)
        whole_ref[pl.ds(start, block.shape[0]), :] = block

    put(chip, core, scaled_ref[...])
    put(1 - chip, core, other_ref[...])
    put(chip, 1 - core, mate_low_ref[...])
    put(chip, 1 - core, mate_high_ref[...], rows // 2)
    put(1 - chip, 1 - core, other_low_ref[...])
    put(1 - chip, 1 - core, other_high_ref[...], rows // 2)
    cot_total = cotangent(place_ref, returned_ref, reward_ref, extra_ref)
    normed = normed_ref[...]
    sigmoid = 1.0 / (1.0 + jnp.exp(-normed))
    slope = sigmoid * (1.0 + normed * (1.0 - sigmoid))
    folded = jnp.dot(weight_ref[...], whole_ref[...], preferred_element_type=jnp.float32)
    d_acted = (
        frame_shift(folded[:rows], 1)
        + folded[rows : 2 * rows]
        + frame_shift(folded[2 * rows :], -1)
    )
    d_normed = by_group(d_acted * slope)
    grouped = by_group(normed)
    result = factor_ref[:, :1, :1] * (
        d_normed - group_mean(d_normed) - grouped * group_mean(d_normed * grouped)
    )
    out_ref[...] = (cot_total + result.reshape(cot_total.shape)).astype(jnp.bfloat16)


def call(kernel, outs, specs, args, scratch=(), cost=0.0, limit=16):
    return pl.pallas_call(
        kernel,
        out_shape=[jax.ShapeDtypeStruct(shape, kind) for shape, kind in outs],
        in_specs=specs,
        out_specs=[VMEM] * len(outs),
        scratch_shapes=list(scratch),
        compiler_params=pltpu.CompilerParams(vmem_limit_bytes=limit * 2**20),
        cost_estimate=pl.CostEstimate(
            flops=int(cost * 1e9), bytes_accessed=int(cost * 1e6), transcendentals=0
        ),
        name=kernel.__name__,
    )(*args)


def local(
    act_carried,
    cot_carried,
    entry_latent,
    reward_head,
    stored_inputs,
    skip_buffer,
    conv_weight,
    time_gain,
    plan,
    timesteps,
):
    sections = lax.axis_size("section")
    section = lax.axis_index("section")
    ch = lax.axis_index("ch")
    rows, cells = act_carried.shape[1:]
    weight = conv_weight[0].reshape(3 * rows, -1)
    full = weight.shape[1]
    stored, skips = stored_inputs[0], skip_buffer[0]
    last = (section == sections - 1).astype(jnp.int32)
    encoder = (section < sections // 2).astype(jnp.int32)
    place = jnp.stack([section, ch % 2, ch // 2, last, encoder])
    field = ((rows, cells), jnp.bfloat16)
    pair = ((2, rows, cells), jnp.float32)

    arrived = shifted(act_carried[0], "section", 1)
    (turned,) = call(transpose_kernel, [((full, 3 * rows), jnp.bfloat16)], [VMEM], [weight], cost=20.0)
    turned, skips, time_gain = lax.optimization_barrier((turned, skips, time_gain))
    gains, added, extra = call(
        prepare_kernel,
        [((2, rows, 128), jnp.float32), field, field],
        [SMEM] * 3 + [VMEM] * 2,
        [place, plan, timesteps, skips, time_gain],
        cost=20.0,
    )
    gains, turned = lax.optimization_barrier((gains, turned))

    mate_side, stacked = call(
        forward_kernel,
        [pair, ((3 * rows, cells), jnp.bfloat16)],
        [SMEM, VMEM, VMEM, VMEM],
        [place, arrived, entry_latent, turned],
    )
    mate_part = swap_core(mate_side)
    cotangents, mate_side = lax.optimization_barrier((cot_carried[0], mate_side))
    returned = shifted(cotangents, "section", -1)
    (own,) = call(own_kernel, [pair], [SMEM, VMEM, VMEM], [place, turned, stacked], cost=20.0)
    near, far_side = call(
        halves_kernel,
        [((rows, cells), jnp.float32), field],
        [SMEM, VMEM, VMEM],
        [place, own, mate_part],
    )
    far = swap_chip(far_side)
    returned, far_side = lax.optimization_barrier((returned, far_side))
    (scaled,) = call(
        scaled_kernel,
        [field],
        [SMEM] + [VMEM] * 4,
        [place, returned, reward_head, extra, gains],
    )
    other = swap_chip(scaled)
    stored, far_side = lax.optimization_barrier((stored, far_side))
    saved_normed, saved_factor = call(
        saved_kernel,
        [((rows, cells), jnp.float32), ((rows // WIDTH, 8, 128), jnp.float32)],
        [SMEM, VMEM],
        [plan, stored],
        cost=20.0,
    )
    far, scaled, saved_normed = lax.optimization_barrier((far, scaled, saved_normed))
    act_out, sent = call(
        output_kernel,
        [field, field],
        [SMEM] + [VMEM] * 8,
        [place, near, far, arrived, entry_latent, added, gains, returned, reward_head],
    )
    mirror_in = lax.ppermute(sent, "section", [(s, sections - 1 - s) for s in range(sections)])

    other, scaled, act_out = lax.optimization_barrier((other, scaled, act_out))
    parts = call(
        split_kernel,
        [((rows // 2, cells), jnp.bfloat16)] * 4,
        [VMEM] * 2,
        [scaled, other],
    )
    mates = [swap_core(part) for part in parts]
    (cot_out,) = call(
        gradient_kernel,
        [field],
        [SMEM] + [VMEM] * 12,
        [
            place,
            saved_normed,
            saved_factor,
            returned,
            reward_head,
            extra,
            scaled,
            other,
            *mates,
            weight,
        ],
        scratch=[pltpu.VMEM((full, cells), jnp.bfloat16)],
    )
    mirror_in, cot_out = lax.optimization_barrier((mirror_in, cot_out))
    return (act_out[None], cot_out[None], mirror_in[None])


def solution(mesh):
    placed = (
        P("section", "ch", None),
        P("section", "ch", None),
        P("ch", None),
        P("ch", None),
        P("section", None, "ch", None),
        P("section", None, "ch", None),
        P("section", None, "ch", None),
        P(None, "ch"),
        P("section", None),
        P("section", None),
    )
    return jax.shard_map(
        local,
        mesh=mesh,
        in_specs=placed,
        out_specs=(P("section", "ch", None), P("section", "ch", None), P("section", "ch", None)),
        check_vma=False,
    )
```

```python
import jax
import jax.numpy as jnp
from jax import lax
from jax.experimental import pallas as pl
from jax.experimental.pallas import tpu as pltpu
from jax.sharding import PartitionSpec as P

C = 1280
GROUPS = 32
CELLS = 64
WIDTH = C // GROUPS

epsilon = 1e-05

VMEM = pl.BlockSpec(memory_space=pltpu.VMEM)
SMEM = pl.BlockSpec(memory_space=pltpu.SMEM)


def shifted(block, axis, distance):
    devices = range(lax.axis_size(axis))
    route = [(i - distance, i) for i in devices if i - distance in devices]
    return lax.ppermute(block, axis, route)


def swap_core(block):
    return lax.ppermute(block, "ch", [(0, 1), (1, 0), (2, 3), (3, 2)])


def swap_chip(block):
    return lax.ppermute(block, "ch", [(0, 2), (2, 0), (1, 3), (3, 1)])


def frame_shift(values, frames_by):
    step = frames_by * CELLS
    if step == 0:
        return values
    width = values.shape[1]
    lane = lax.broadcasted_iota(jnp.int32, values.shape, 1)
    rolled = pltpu.roll(values, (-step) % width, 1)
    kept = lane < width - step if step > 0 else lane >= -step
    return jnp.where(kept, rolled, 0.0)


def group_mean(grouped):
    total = jnp.sum(jnp.sum(grouped, axis=1, keepdims=True), axis=2, keepdims=True)
    return total * (1.0 / (grouped.shape[1] * grouped.shape[2]))


def by_group(values):
    return values.reshape(values.shape[0] // WIDTH, WIDTH, values.shape[1])


def normalize(values):
    grouped = by_group(values)
    centred = grouped - group_mean(grouped)
    factor = lax.rsqrt(group_mean(centred * centred) + epsilon)
    return (centred * factor).reshape(values.shape), factor


def column(table_ref, stamp):
    width = table_ref.shape[1]
    row = jnp.broadcast_to(table_ref[pl.ds(stamp, 1), :], (width, width))
    across = lax.broadcasted_iota(jnp.int32, (width, width), 0)
    along = lax.broadcasted_iota(jnp.int32, (width, width), 1)
    return jnp.sum(jnp.where(across == along, row, 0.0), axis=1, keepdims=True)


def transpose_kernel(weight_ref, out_ref):
    depth = weight_ref.shape[0]
    for start in range(0, depth, 128):
        size = min(128, depth - start)
        out_ref[:, start : start + size] = weight_ref[start : start + size, :].T


def forward_kernel(place_ref, arrived_ref, entry_ref, weight_ref, mate_ref, stacked_ref):
    rows = arrived_ref.shape[0]
    first = place_ref[0] == 0
    x_in = jnp.where(first, entry_ref[...], arrived_ref[...]).astype(jnp.float32)
    normed, _ = normalize(x_in)
    acted = normed / (1.0 + jnp.exp(-normed))
    for k in range(3):
        stacked_ref[k * rows : (k + 1) * rows, :] = frame_shift(acted, k - 1).astype(jnp.bfloat16)
    own_side(1 - place_ref[1], weight_ref, stacked_ref, mate_ref)


def own_side(core, weight_ref, stacked_ref, out_ref):
    rows = out_ref.shape[1]
    for chip in range(2):
        start = pl.multiple_of((chip * 2 + core) * rows, rows)
        out_ref[chip] = jnp.dot(
            weight_ref[pl.ds(start, rows), :], stacked_ref[...], preferred_element_type=jnp.float32
        )


def own_kernel(place_ref, weight_ref, stacked_ref, own_ref):
    own_side(place_ref[1], weight_ref, stacked_ref, own_ref)


def prepare_kernel(
    place_ref, plan_ref, stamps_ref, skip_ref, gain_ref, columns_ref, added_ref, extra_ref
):
    for way in range(2):
        columns_ref[way] = jnp.broadcast_to(
            column(gain_ref, stamps_ref[0, way]), columns_ref.shape[1:]
        )
    encoder = place_ref[4] == 1
    added = skip_ref[plan_ref[0, 0]]
    extra = skip_ref[plan_ref[0, 1]]
    added_ref[...] = jnp.where(encoder, jnp.zeros_like(added), added)
    extra_ref[...] = jnp.where(encoder, extra, jnp.zeros_like(extra))


def cotangent(place_ref, returned_ref, reward_ref, extra_ref):
    cot_in = jnp.where(place_ref[3] == 1, reward_ref[...], returned_ref[...])
    return cot_in.astype(jnp.float32) + extra_ref[...].astype(jnp.float32)


def scaled_kernel(place_ref, returned_ref, reward_ref, extra_ref, columns_ref, scaled_ref):
    cot_total = cotangent(place_ref, returned_ref, reward_ref, extra_ref)
    scaled_ref[...] = (cot_total * columns_ref[1][:, :1]).astype(jnp.bfloat16)


def halves_kernel(place_ref, own_ref, mate_ref, near_ref, far_ref):
    chip = place_ref[2]
    near_ref[...] = own_ref[chip] + mate_ref[chip]
    far_ref[...] = (own_ref[1 - chip] + mate_ref[1 - chip]).astype(jnp.bfloat16)


def output_kernel(
    place_ref,
    near_ref,
    far_ref,
    arrived_ref,
    entry_ref,
    added_ref,
    columns_ref,
    cot_ref,
    reward_ref,
    out_ref,
    sent_ref,
):
    x_in = jnp.where(place_ref[0] == 0, entry_ref[...], arrived_ref[...]).astype(jnp.float32)
    conv_sum = near_ref[...] + far_ref[...].astype(jnp.float32)
    act_out = x_in + conv_sum * columns_ref[0][:, :1] + added_ref[...].astype(jnp.float32)
    act_out = act_out.astype(jnp.bfloat16)
    out_ref[...] = act_out
    cot_in = jnp.where(place_ref[5] == 1, reward_ref[...], cot_ref[...])
    rows = out_ref.shape[0]
    sent_ref[rows:, :] = jnp.zeros((sent_ref.shape[0] - rows, sent_ref.shape[1]), jnp.bfloat16)
    sent_ref[:rows, :] = jnp.where(place_ref[4] == 1, act_out, cot_in)


def saved_kernel(plan_ref, stored_ref, normed_ref, factor_ref):
    normed, factor = normalize(stored_ref[plan_ref[0, 1]].astype(jnp.float32))
    normed_ref[...] = normed
    factor_ref[...] = jnp.broadcast_to(factor, factor_ref.shape)


def gradient_kernel(
    place_ref, normed_ref, factor_ref, returned_ref, reward_ref, extra_ref, *refs
):
    *part_refs, weight_ref, out_ref, whole_ref = refs
    rows = out_ref.shape[0]
    ch = place_ref[1] + 2 * place_ref[2]
    for k in range(4):
        start = jnp.bitwise_xor(ch, k) * rows
        whole_ref[pl.ds(pl.multiple_of(start, rows), rows), :] = part_refs[k][...]
    cot_total = cotangent(place_ref, returned_ref, reward_ref, extra_ref)
    normed = normed_ref[...]
    sigmoid = 1.0 / (1.0 + jnp.exp(-normed))
    slope = sigmoid * (1.0 + normed * (1.0 - sigmoid))
    folded = jnp.dot(weight_ref[...], whole_ref[...], preferred_element_type=jnp.float32)
    d_acted = (
        frame_shift(folded[:rows], 1)
        + folded[rows : 2 * rows]
        + frame_shift(folded[2 * rows :], -1)
    )
    d_normed = by_group(d_acted * slope)
    grouped = by_group(normed)
    result = factor_ref[:, :1, :1] * (
        d_normed - group_mean(d_normed) - grouped * group_mean(d_normed * grouped)
    )
    out_ref[...] = (cot_total + result.reshape(cot_total.shape)).astype(jnp.bfloat16)


def call(kernel, outs, specs, args, scratch=(), cost=0.0, limit=16):
    return pl.pallas_call(
        kernel,
        out_shape=[jax.ShapeDtypeStruct(shape, kind) for shape, kind in outs],
        in_specs=specs,
        out_specs=[VMEM] * len(outs),
        scratch_shapes=list(scratch),
        compiler_params=pltpu.CompilerParams(vmem_limit_bytes=limit * 2**20),
        cost_estimate=pl.CostEstimate(
            flops=int(cost * 1e9), bytes_accessed=int(cost * 1e6), transcendentals=0
        ),
        name=kernel.__name__,
    )(*args)


def local(
    act_carried,
    cot_carried,
    entry_latent,
    reward_head,
    stored_inputs,
    skip_buffer,
    conv_weight,
    time_gain,
    plan,
    timesteps,
):
    sections = lax.axis_size("section")
    section = lax.axis_index("section")
    ch = lax.axis_index("ch")
    rows, cells = act_carried.shape[1:]
    weight = conv_weight[0].reshape(3 * rows, -1)
    full = weight.shape[1]
    stored, skips = stored_inputs[0], skip_buffer[0]
    last = (section == sections - 1).astype(jnp.int32)
    encoder = (section < sections // 2).astype(jnp.int32)
    middle = (section == sections // 2).astype(jnp.int32)
    place = jnp.stack([section, ch % 2, ch // 2, last, encoder, middle])
    field = ((rows, cells), jnp.bfloat16)
    pair = ((2, rows, cells), jnp.float32)

    arrived = shifted(act_carried[0], "section", 1)
    (turned,) = call(transpose_kernel, [((full, 3 * rows), jnp.bfloat16)], [VMEM], [weight], cost=20.0)
    turned, skips, time_gain = lax.optimization_barrier((turned, skips, time_gain))
    gains, added, extra = call(
        prepare_kernel,
        [((2, rows, 128), jnp.float32), field, field],
        [SMEM] * 3 + [VMEM] * 2,
        [place, plan, timesteps, skips, time_gain],
        cost=20.0,
    )
    gains, turned = lax.optimization_barrier((gains, turned))

    mate_side, stacked = call(
        forward_kernel,
        [pair, ((3 * rows, cells), jnp.bfloat16)],
        [SMEM, VMEM, VMEM, VMEM],
        [place, arrived, entry_latent, turned],
    )
    mate_part = swap_core(mate_side)
    (own,) = call(own_kernel, [pair], [SMEM, VMEM, VMEM], [place, turned, stacked], cost=20.0)
    near, far_side = call(
        halves_kernel,
        [((rows, cells), jnp.float32), field],
        [SMEM, VMEM, VMEM],
        [place, own, mate_part],
    )
    far = swap_chip(far_side)
    cotangents, far_side = lax.optimization_barrier((cot_carried[0], far_side))
    returned = shifted(cotangents, "section", -1)
    stored, far_side = lax.optimization_barrier((stored, far_side))
    saved_normed, saved_factor = call(
        saved_kernel,
        [((rows, cells), jnp.float32), ((rows // WIDTH, 8, 128), jnp.float32)],
        [SMEM, VMEM],
        [plan, stored],
        cost=20.0,
    )
    far, saved_normed = lax.optimization_barrier((far, saved_normed))
    act_out, sent = call(
        output_kernel,
        [field, ((rows + 16, cells), jnp.bfloat16)],
        [SMEM] + [VMEM] * 8,
        [place, near, far, arrived, entry_latent, added, gains, cot_carried[0], reward_head],
    )
    half = sections // 2
    route = [(s, sections - 1 - s) for s in range(half)]
    route += [(s, (sections - s) % half) for s in range(half, sections)]
    mirror_in = lax.ppermute(sent, "section", route)[:rows]

    returned, act_out = lax.optimization_barrier((returned, act_out))
    (scaled,) = call(
        scaled_kernel,
        [field],
        [SMEM] + [VMEM] * 4,
        [place, returned, reward_head, extra, gains],
    )
    gathered = [lax.ppermute(scaled, "ch", [(c, c ^ k) for c in range(4)]) for k in (1, 2, 3)]
    (cot_out,) = call(
        gradient_kernel,
        [field],
        [SMEM] + [VMEM] * 10,
        [
            place,
            saved_normed,
            saved_factor,
            returned,
            reward_head,
            extra,
            scaled,
            *gathered,
            weight,
        ],
        scratch=[pltpu.VMEM((full, cells), jnp.bfloat16)],
    )
    mirror_in, cot_out = lax.optimization_barrier((mirror_in, cot_out))
    return (act_out[None], cot_out[None], mirror_in[None])


def solution(mesh):
    placed = (
        P("section", "ch", None),
        P("section", "ch", None),
        P("ch", None),
        P("ch", None),
        P("section", None, "ch", None),
        P("section", None, "ch", None),
        P("section", None, "ch", None),
        P(None, "ch"),
        P("section", None),
        P("section", None),
    )
    return jax.shard_map(
        local,
        mesh=mesh,
        in_specs=placed,
        out_specs=(P("section", "ch", None), P("section", "ch", None), P("section", "ch", None)),
        check_vma=False,
    )
```

```python
import jax
import jax.numpy as jnp
from jax import lax
from jax.experimental import pallas as pl
from jax.experimental.pallas import tpu as pltpu
from jax.sharding import PartitionSpec as P

C = 1280
GROUPS = 32
CELLS = 64
WIDTH = C // GROUPS

epsilon = 1e-05

VMEM = pl.BlockSpec(memory_space=pltpu.VMEM)
SMEM = pl.BlockSpec(memory_space=pltpu.SMEM)


def shifted(block, axis, distance):
    devices = range(lax.axis_size(axis))
    route = [(i - distance, i) for i in devices if i - distance in devices]
    return lax.ppermute(block, axis, route)


def swap_core(block):
    return lax.ppermute(block, "ch", [(0, 1), (1, 0), (2, 3), (3, 2)])


def swap_chip(block):
    return lax.ppermute(block, "ch", [(0, 2), (2, 0), (1, 3), (3, 1)])


def frame_shift(values, frames_by):
    step = frames_by * CELLS
    if step == 0:
        return values
    width = values.shape[1]
    lane = lax.broadcasted_iota(jnp.int32, values.shape, 1)
    rolled = pltpu.roll(values, (-step) % width, 1)
    kept = lane < width - step if step > 0 else lane >= -step
    return jnp.where(kept, rolled, 0.0)


def group_mean(grouped):
    total = jnp.sum(jnp.sum(grouped, axis=1, keepdims=True), axis=2, keepdims=True)
    return total * (1.0 / (grouped.shape[1] * grouped.shape[2]))


def by_group(values):
    return values.reshape(values.shape[0] // WIDTH, WIDTH, values.shape[1])


def normalize(values):
    grouped = by_group(values)
    centred = grouped - group_mean(grouped)
    factor = lax.rsqrt(group_mean(centred * centred) + epsilon)
    return (centred * factor).reshape(values.shape), factor


def column(table_ref, stamp):
    width = table_ref.shape[1]
    row = jnp.broadcast_to(table_ref[pl.ds(stamp, 1), :], (width, width))
    across = lax.broadcasted_iota(jnp.int32, (width, width), 0)
    along = lax.broadcasted_iota(jnp.int32, (width, width), 1)
    return jnp.sum(jnp.where(across == along, row, 0.0), axis=1, keepdims=True)


def transpose_kernel(weight_ref, out_ref):
    depth = weight_ref.shape[0]
    for start in range(0, depth, 128):
        size = min(128, depth - start)
        out_ref[:, start : start + size] = weight_ref[start : start + size, :].T


def forward_kernel(place_ref, arrived_ref, entry_ref, weight_ref, mate_ref, stacked_ref):
    rows = arrived_ref.shape[0]
    first = place_ref[0] == 0
    x_in = jnp.where(first, entry_ref[...], arrived_ref[...]).astype(jnp.float32)
    normed, _ = normalize(x_in)
    acted = normed / (1.0 + jnp.exp(-normed))
    for k in range(3):
        stacked_ref[k * rows : (k + 1) * rows, :] = frame_shift(acted, k - 1).astype(jnp.bfloat16)
    own_side(1 - place_ref[1], weight_ref, stacked_ref, mate_ref)


def own_side(core, weight_ref, stacked_ref, out_ref):
    rows = out_ref.shape[1]
    for chip in range(2):
        start = pl.multiple_of((chip * 2 + core) * rows, rows)
        out_ref[chip] = jnp.dot(
            weight_ref[pl.ds(start, rows), :], stacked_ref[...], preferred_element_type=jnp.float32
        )


def own_kernel(place_ref, weight_ref, stacked_ref, own_ref):
    own_side(place_ref[1], weight_ref, stacked_ref, own_ref)


def prepare_kernel(
    place_ref, plan_ref, stamps_ref, skip_ref, gain_ref, columns_ref, added_ref, extra_ref
):
    for way in range(2):
        columns_ref[way] = jnp.broadcast_to(
            column(gain_ref, stamps_ref[0, way]), columns_ref.shape[1:]
        )
    encoder = place_ref[4] == 1
    added = skip_ref[plan_ref[0, 0]]
    extra = skip_ref[plan_ref[0, 1]]
    added_ref[...] = jnp.where(encoder, jnp.zeros_like(added), added)
    extra_ref[...] = jnp.where(encoder, extra, jnp.zeros_like(extra))


def cotangent(place_ref, returned_ref, reward_ref, extra_ref):
    cot_in = jnp.where(place_ref[3] == 1, reward_ref[...], returned_ref[...])
    return cot_in.astype(jnp.float32) + extra_ref[...].astype(jnp.float32)


def scaled_kernel(place_ref, returned_ref, reward_ref, extra_ref, columns_ref, scaled_ref):
    cot_total = cotangent(place_ref, returned_ref, reward_ref, extra_ref)
    scaled_ref[...] = (cot_total * columns_ref[1][:, :1]).astype(jnp.bfloat16)


def halves_kernel(place_ref, own_ref, mate_ref, near_ref, far_ref):
    chip = place_ref[2]
    near_ref[...] = own_ref[chip] + mate_ref[chip]
    far_ref[...] = (own_ref[1 - chip] + mate_ref[1 - chip]).astype(jnp.bfloat16)


def output_kernel(
    place_ref,
    near_ref,
    far_ref,
    arrived_ref,
    entry_ref,
    added_ref,
    columns_ref,
    cot_ref,
    reward_ref,
    out_ref,
    sent_ref,
):
    x_in = jnp.where(place_ref[0] == 0, entry_ref[...], arrived_ref[...]).astype(jnp.float32)
    conv_sum = near_ref[...] + far_ref[...].astype(jnp.float32)
    act_out = x_in + conv_sum * columns_ref[0][:, :1] + added_ref[...].astype(jnp.float32)
    act_out = act_out.astype(jnp.bfloat16)
    out_ref[...] = act_out
    cot_in = jnp.where(place_ref[5] == 1, reward_ref[...], cot_ref[...])
    sent_ref[...] = jnp.where(place_ref[4] == 1, act_out, cot_in)


def saved_kernel(plan_ref, stored_ref, normed_ref, factor_ref):
    normed, factor = normalize(stored_ref[plan_ref[0, 1]].astype(jnp.float32))
    normed_ref[...] = normed
    factor_ref[...] = jnp.broadcast_to(factor, factor_ref.shape)


def split_kernel(scaled_ref, other_ref, *part_refs):
    half = part_refs[0].shape[0]
    for i, part_ref in enumerate(part_refs):
        source_ref = (scaled_ref, other_ref)[i // 2]
        part_ref[...] = source_ref[i % 2 * half : (i % 2 + 1) * half, :]


def gradient_kernel(
    place_ref,
    normed_ref,
    factor_ref,
    returned_ref,
    reward_ref,
    extra_ref,
    scaled_ref,
    other_ref,
    mate_low_ref,
    mate_high_ref,
    other_low_ref,
    other_high_ref,
    weight_ref,
    out_ref,
    whole_ref,
):
    rows = scaled_ref.shape[0]
    core, chip = place_ref[1], place_ref[2]

    def put(chip, core, block, skipped=0):
        start = pl.multiple_of((chip * 2 + core) * rows + skipped, 32)
        whole_ref[pl.ds(start, block.shape[0]), :] = block

    put(chip, core, scaled_ref[...])
    put(1 - chip, core, other_ref[...])
    put(chip, 1 - core, mate_low_ref[...])
    put(chip, 1 - core, mate_high_ref[...], rows // 2)
    put(1 - chip, 1 - core, other_low_ref[...])
    put(1 - chip, 1 - core, other_high_ref[...], rows // 2)
    cot_total = cotangent(place_ref, returned_ref, reward_ref, extra_ref)
    normed = normed_ref[...]
    sigmoid = 1.0 / (1.0 + jnp.exp(-normed))
    slope = sigmoid * (1.0 + normed * (1.0 - sigmoid))
    folded = jnp.dot(weight_ref[...], whole_ref[...], preferred_element_type=jnp.float32)
    d_acted = (
        frame_shift(folded[:rows], 1)
        + folded[rows : 2 * rows]
        + frame_shift(folded[2 * rows :], -1)
    )
    d_normed = by_group(d_acted * slope)
    grouped = by_group(normed)
    result = factor_ref[:, :1, :1] * (
        d_normed - group_mean(d_normed) - grouped * group_mean(d_normed * grouped)
    )
    out_ref[...] = (cot_total + result.reshape(cot_total.shape)).astype(jnp.bfloat16)


def call(kernel, outs, specs, args, scratch=(), cost=0.0, limit=16):
    return pl.pallas_call(
        kernel,
        out_shape=[jax.ShapeDtypeStruct(shape, kind) for shape, kind in outs],
        in_specs=specs,
        out_specs=[VMEM] * len(outs),
        scratch_shapes=list(scratch),
        compiler_params=pltpu.CompilerParams(vmem_limit_bytes=limit * 2**20),
        cost_estimate=pl.CostEstimate(
            flops=int(cost * 1e9), bytes_accessed=int(cost * 1e6), transcendentals=0
        ),
        name=kernel.__name__,
    )(*args)


def local(
    act_carried,
    cot_carried,
    entry_latent,
    reward_head,
    stored_inputs,
    skip_buffer,
    conv_weight,
    time_gain,
    plan,
    timesteps,
):
    sections = lax.axis_size("section")
    section = lax.axis_index("section")
    ch = lax.axis_index("ch")
    rows, cells = act_carried.shape[1:]
    weight = conv_weight[0].reshape(3 * rows, -1)
    full = weight.shape[1]
    stored, skips = stored_inputs[0], skip_buffer[0]
    last = (section == sections - 1).astype(jnp.int32)
    encoder = (section < sections // 2).astype(jnp.int32)
    middle = (section == sections // 2).astype(jnp.int32)
    place = jnp.stack([section, ch % 2, ch // 2, last, encoder, middle])
    field = ((rows, cells), jnp.bfloat16)
    pair = ((2, rows, cells), jnp.float32)

    arrived = shifted(act_carried[0], "section", 1)
    (turned,) = call(transpose_kernel, [((full, 3 * rows), jnp.bfloat16)], [VMEM], [weight], cost=20.0)
    turned, skips, time_gain = lax.optimization_barrier((turned, skips, time_gain))
    gains, added, extra = call(
        prepare_kernel,
        [((2, rows, 128), jnp.float32), field, field],
        [SMEM] * 3 + [VMEM] * 2,
        [place, plan, timesteps, skips, time_gain],
        cost=20.0,
    )
    cotangents, gains, turned = lax.optimization_barrier((cot_carried[0], gains, turned))
    returned = shifted(cotangents, "section", -1)

    mate_side, stacked = call(
        forward_kernel,
        [pair, ((3 * rows, cells), jnp.bfloat16)],
        [SMEM, VMEM, VMEM, VMEM],
        [place, arrived, entry_latent, turned],
    )
    mate_part = swap_core(mate_side)
    (own,) = call(own_kernel, [pair], [SMEM, VMEM, VMEM], [place, turned, stacked], cost=20.0)
    near, far_side = call(
        halves_kernel,
        [((rows, cells), jnp.float32), field],
        [SMEM, VMEM, VMEM],
        [place, own, mate_part],
    )
    far = swap_chip(far_side)
    returned, far_side = lax.optimization_barrier((returned, far_side))
    (scaled,) = call(
        scaled_kernel,
        [field],
        [SMEM] + [VMEM] * 4,
        [place, returned, reward_head, extra, gains],
    )
    other = swap_chip(scaled)
    stored, far_side = lax.optimization_barrier((stored, far_side))
    saved_normed, saved_factor = call(
        saved_kernel,
        [((rows, cells), jnp.float32), ((rows // WIDTH, 8, 128), jnp.float32)],
        [SMEM, VMEM],
        [plan, stored],
        cost=20.0,
    )
    far, scaled, saved_normed = lax.optimization_barrier((far, scaled, saved_normed))
    act_out, sent = call(
        output_kernel,
        [field, field],
        [SMEM] + [VMEM] * 8,
        [place, near, far, arrived, entry_latent, added, gains, cot_carried[0], reward_head],
    )
    half = sections // 2
    route = [(s, sections - 1 - s) for s in range(half)]
    route += [(s, (sections - s) % half) for s in range(half, sections)]
    mirror_in = lax.ppermute(sent, "section", route)

    other, scaled, act_out = lax.optimization_barrier((other, scaled, act_out))
    parts = call(
        split_kernel,
        [((rows // 2, cells), jnp.bfloat16)] * 4,
        [VMEM] * 2,
        [scaled, other],
    )
    mates = [swap_core(part) for part in parts]
    (cot_out,) = call(
        gradient_kernel,
        [field],
        [SMEM] + [VMEM] * 12,
        [
            place,
            saved_normed,
            saved_factor,
            returned,
            reward_head,
            extra,
            scaled,
            other,
            *mates,
            weight,
        ],
        scratch=[pltpu.VMEM((full, cells), jnp.bfloat16)],
    )
    mirror_in, cot_out = lax.optimization_barrier((mirror_in, cot_out))
    return (act_out[None], cot_out[None], mirror_in[None])


def solution(mesh):
    placed = (
        P("section", "ch", None),
        P("section", "ch", None),
        P("ch", None),
        P("ch", None),
        P("section", None, "ch", None),
        P("section", None, "ch", None),
        P("section", None, "ch", None),
        P(None, "ch"),
        P("section", None),
        P("section", None),
    )
    return jax.shard_map(
        local,
        mesh=mesh,
        in_specs=placed,
        out_specs=(P("section", "ch", None), P("section", "ch", None), P("section", "ch", None)),
        check_vma=False,
    )
```

```python
import jax
import jax.numpy as jnp
from jax import lax
from jax.experimental import pallas as pl
from jax.experimental.pallas import tpu as pltpu
from jax.sharding import PartitionSpec as P

C = 1280
GROUPS = 32
CELLS = 64
WIDTH = C // GROUPS

epsilon = 1e-05

VMEM = pl.BlockSpec(memory_space=pltpu.VMEM)
SMEM = pl.BlockSpec(memory_space=pltpu.SMEM)


def shifted(block, axis, distance):
    devices = range(lax.axis_size(axis))
    route = [(i - distance, i) for i in devices if i - distance in devices]
    return lax.ppermute(block, axis, route)


def swap_core(block):
    return lax.ppermute(block, "ch", [(0, 1), (1, 0), (2, 3), (3, 2)])


def swap_chip(block):
    return lax.ppermute(block, "ch", [(0, 2), (2, 0), (1, 3), (3, 1)])


def frame_shift(values, frames_by):
    step = frames_by * CELLS
    if step == 0:
        return values
    width = values.shape[1]
    lane = lax.broadcasted_iota(jnp.int32, values.shape, 1)
    rolled = pltpu.roll(values, (-step) % width, 1)
    kept = lane < width - step if step > 0 else lane >= -step
    return jnp.where(kept, rolled, 0.0)


def group_mean(grouped):
    total = jnp.sum(jnp.sum(grouped, axis=1, keepdims=True), axis=2, keepdims=True)
    return total * (1.0 / (grouped.shape[1] * grouped.shape[2]))


def by_group(values):
    return values.reshape(values.shape[0] // WIDTH, WIDTH, values.shape[1])


def normalize(values):
    grouped = by_group(values)
    centred = grouped - group_mean(grouped)
    factor = lax.rsqrt(group_mean(centred * centred) + epsilon)
    return (centred * factor).reshape(values.shape), factor


def column(table_ref, stamp):
    width = table_ref.shape[1]
    row = jnp.broadcast_to(table_ref[pl.ds(stamp, 1), :], (width, width))
    across = lax.broadcasted_iota(jnp.int32, (width, width), 0)
    along = lax.broadcasted_iota(jnp.int32, (width, width), 1)
    return jnp.sum(jnp.where(across == along, row, 0.0), axis=1, keepdims=True)


def transpose_kernel(weight_ref, out_ref):
    depth = weight_ref.shape[0]
    for start in range(0, depth, 128):
        size = min(128, depth - start)
        out_ref[:, start : start + size] = weight_ref[start : start + size, :].T


def forward_kernel(place_ref, arrived_ref, entry_ref, weight_ref, mate_ref, stacked_ref):
    rows = arrived_ref.shape[0]
    first = place_ref[0] == 0
    x_in = jnp.where(first, entry_ref[...], arrived_ref[...]).astype(jnp.float32)
    normed, _ = normalize(x_in)
    acted = normed / (1.0 + jnp.exp(-normed))
    for k in range(3):
        stacked_ref[k * rows : (k + 1) * rows, :] = frame_shift(acted, k - 1).astype(jnp.bfloat16)
    own_side(1 - place_ref[1], weight_ref, stacked_ref, mate_ref)


def own_side(core, weight_ref, stacked_ref, out_ref):
    rows = out_ref.shape[1]
    for chip in range(2):
        start = pl.multiple_of((chip * 2 + core) * rows, rows)
        out_ref[chip] = jnp.dot(
            weight_ref[pl.ds(start, rows), :], stacked_ref[...], preferred_element_type=jnp.float32
        )


def own_kernel(place_ref, weight_ref, stacked_ref, own_ref):
    own_side(place_ref[1], weight_ref, stacked_ref, own_ref)


def prepare_kernel(
    place_ref, plan_ref, stamps_ref, skip_ref, gain_ref, columns_ref, added_ref, extra_ref
):
    for way in range(2):
        columns_ref[way] = jnp.broadcast_to(
            column(gain_ref, stamps_ref[0, way]), columns_ref.shape[1:]
        )
    encoder = place_ref[4] == 1
    added = skip_ref[plan_ref[0, 0]]
    extra = skip_ref[plan_ref[0, 1]]
    added_ref[...] = jnp.where(encoder, jnp.zeros_like(added), added)
    extra_ref[...] = jnp.where(encoder, extra, jnp.zeros_like(extra))


def cotangent(place_ref, returned_ref, reward_ref, extra_ref):
    cot_in = jnp.where(place_ref[3] == 1, reward_ref[...], returned_ref[...])
    return cot_in.astype(jnp.float32) + extra_ref[...].astype(jnp.float32)


def scaled_kernel(place_ref, returned_ref, reward_ref, extra_ref, columns_ref, scaled_ref):
    cot_total = cotangent(place_ref, returned_ref, reward_ref, extra_ref)
    scaled_ref[...] = gained(cot_total, columns_ref, 1).astype(jnp.bfloat16)


def halves_kernel(place_ref, own_ref, mate_ref, far_ref):
    chip = 1 - place_ref[2]
    far_ref[...] = (own_ref[chip] + mate_ref[chip]).astype(jnp.bfloat16)


def gained(values, columns_ref, way):
    size = columns_ref.shape[2]
    return jnp.concatenate(
        [
            values[:, start : start + size] * columns_ref[way]
            for start in range(0, values.shape[1], size)
        ],
        1,
    )


def near_kernel(
    place_ref,
    plan_ref,
    own_ref,
    mate_ref,
    arrived_ref,
    entry_ref,
    added_ref,
    columns_ref,
    stored_ref,
    near_ref,
    normed_ref,
    factor_ref,
):
    chip = place_ref[2]
    x_in = jnp.where(place_ref[0] == 0, entry_ref[...], arrived_ref[...]).astype(jnp.float32)
    near = gained(own_ref[chip] + mate_ref[chip], columns_ref, 0)
    near_ref[...] = x_in + near + added_ref[...].astype(jnp.float32)
    normed, factor = normalize(stored_ref[plan_ref[0, 1]].astype(jnp.float32))
    normed_ref[...] = normed
    factor_ref[...] = jnp.broadcast_to(factor, factor_ref.shape)


def output_kernel(near_ref, far_ref, columns_ref, out_ref):
    far = gained(far_ref[...].astype(jnp.float32), columns_ref, 0)
    out_ref[...] = (near_ref[...] + far).astype(jnp.bfloat16)


def sent_kernel(place_ref, near_ref, far_ref, columns_ref, cot_ref, reward_ref, sent_ref):
    @pl.when(place_ref[4] == 1)
    def _():
        output_kernel(near_ref, far_ref, columns_ref, sent_ref)

    @pl.when(place_ref[5] == 1)
    def _():
        sent_ref[...] = reward_ref[...]

    @pl.when(place_ref[4] + place_ref[5] == 0)
    def _():
        sent_ref[...] = cot_ref[...]


def split_kernel(scaled_ref, other_ref, *part_refs):
    half = part_refs[0].shape[0]
    for i, part_ref in enumerate(part_refs):
        source_ref = (scaled_ref, other_ref)[i // 2]
        part_ref[...] = source_ref[i % 2 * half : (i % 2 + 1) * half, :]


def gradient_kernel(
    place_ref,
    normed_ref,
    factor_ref,
    returned_ref,
    reward_ref,
    extra_ref,
    scaled_ref,
    other_ref,
    mate_low_ref,
    mate_high_ref,
    other_low_ref,
    other_high_ref,
    weight_ref,
    out_ref,
    whole_ref,
):
    rows = scaled_ref.shape[0]
    core, chip = place_ref[1], place_ref[2]

    def put(chip, core, block, skipped=0):
        start = pl.multiple_of((chip * 2 + core) * rows + skipped, 32)
        whole_ref[pl.ds(start, block.shape[0]), :] = block

    put(chip, core, scaled_ref[...])
    put(1 - chip, core, other_ref[...])
    put(chip, 1 - core, mate_low_ref[...])
    put(chip, 1 - core, mate_high_ref[...], rows // 2)
    put(1 - chip, 1 - core, other_low_ref[...])
    put(1 - chip, 1 - core, other_high_ref[...], rows // 2)
    cot_total = cotangent(place_ref, returned_ref, reward_ref, extra_ref)
    normed = normed_ref[...]
    sigmoid = 1.0 / (1.0 + jnp.exp(-normed))
    slope = sigmoid * (1.0 + normed * (1.0 - sigmoid))
    folded = jnp.dot(weight_ref[...], whole_ref[...], preferred_element_type=jnp.float32)
    d_acted = (
        frame_shift(folded[:rows], 1)
        + folded[rows : 2 * rows]
        + frame_shift(folded[2 * rows :], -1)
    )
    d_normed = by_group(d_acted * slope)
    grouped = by_group(normed)
    result = factor_ref[:, :1, :1] * (
        d_normed - group_mean(d_normed) - grouped * group_mean(d_normed * grouped)
    )
    out_ref[...] = (cot_total + result.reshape(cot_total.shape)).astype(jnp.bfloat16)


def call(kernel, outs, specs, args, scratch=(), cost=0.0, limit=16):
    return pl.pallas_call(
        kernel,
        out_shape=[jax.ShapeDtypeStruct(shape, kind) for shape, kind in outs],
        in_specs=specs,
        out_specs=[VMEM] * len(outs),
        scratch_shapes=list(scratch),
        compiler_params=pltpu.CompilerParams(vmem_limit_bytes=limit * 2**20),
        cost_estimate=pl.CostEstimate(
            flops=int(cost * 1e9), bytes_accessed=int(cost * 1e6), transcendentals=0
        ),
        name=kernel.__name__,
    )(*args)


def local(
    act_carried,
    cot_carried,
    entry_latent,
    reward_head,
    stored_inputs,
    skip_buffer,
    conv_weight,
    time_gain,
    plan,
    timesteps,
):
    sections = lax.axis_size("section")
    section = lax.axis_index("section")
    ch = lax.axis_index("ch")
    rows, cells = act_carried.shape[1:]
    weight = conv_weight[0].reshape(3 * rows, -1)
    full = weight.shape[1]
    stored, skips = stored_inputs[0], skip_buffer[0]
    last = (section == sections - 1).astype(jnp.int32)
    encoder = (section < sections // 2).astype(jnp.int32)
    middle = (section == sections // 2).astype(jnp.int32)
    place = jnp.stack([section, ch % 2, ch // 2, last, encoder, middle])
    field = ((rows, cells), jnp.bfloat16)
    pair = ((2, rows, cells), jnp.float32)

    arrived = shifted(act_carried[0], "section", 1)
    (turned,) = call(transpose_kernel, [((full, 3 * rows), jnp.bfloat16)], [VMEM], [weight], cost=20.0)
    turned, skips, time_gain = lax.optimization_barrier((turned, skips, time_gain))
    gains, added, extra = call(
        prepare_kernel,
        [((2, rows, 128), jnp.float32), field, field],
        [SMEM] * 3 + [VMEM] * 2,
        [place, plan, timesteps, skips, time_gain],
        cost=20.0,
    )
    cotangents, gains, turned = lax.optimization_barrier((cot_carried[0], gains, turned))
    returned = shifted(cotangents, "section", -1)

    mate_side, stacked = call(
        forward_kernel,
        [pair, ((3 * rows, cells), jnp.bfloat16)],
        [SMEM, VMEM, VMEM, VMEM],
        [place, arrived, entry_latent, turned],
    )
    mate_part = swap_core(mate_side)
    (own,) = call(own_kernel, [pair], [SMEM, VMEM, VMEM], [place, turned, stacked], cost=20.0)
    (far_side,) = call(halves_kernel, [field], [SMEM, VMEM, VMEM], [place, own, mate_part])
    far = swap_chip(far_side)
    stored, far_side = lax.optimization_barrier((stored, far_side))
    whole = ((rows, cells), jnp.float32)
    near, saved_normed, saved_factor = call(
        near_kernel,
        [whole, whole, ((rows // WIDTH, 8, 128), jnp.float32)],
        [SMEM] * 2 + [VMEM] * 7,
        [place, plan, own, mate_part, arrived, entry_latent, added, gains, stored],
        cost=20.0,
    )
    returned, near = lax.optimization_barrier((returned, near))
    (scaled,) = call(
        scaled_kernel,
        [field],
        [SMEM] + [VMEM] * 4,
        [place, returned, reward_head, extra, gains],
    )
    other = swap_chip(scaled)
    far, scaled = lax.optimization_barrier((far, scaled))
    (sent,) = call(
        sent_kernel,
        [field],
        [SMEM] + [VMEM] * 5,
        [place, near, far, gains, cot_carried[0], reward_head],
    )
    half = sections // 2
    route = [(s, sections - 1 - s) for s in range(half)]
    route += [(s, (sections - s) % half) for s in range(half, sections)]
    mirror_in = lax.ppermute(sent, "section", route)

    other, scaled, near, sent = lax.optimization_barrier((other, scaled, near, sent))
    (act_out,) = call(output_kernel, [field], [VMEM] * 3, [near, far, gains])
    parts = call(
        split_kernel,
        [((rows // 2, cells), jnp.bfloat16)] * 4,
        [VMEM] * 2,
        [scaled, other],
    )
    mates = [swap_core(part) for part in parts]
    (cot_out,) = call(
        gradient_kernel,
        [field],
        [SMEM] + [VMEM] * 12,
        [
            place,
            saved_normed,
            saved_factor,
            returned,
            reward_head,
            extra,
            scaled,
            other,
            *mates,
            weight,
        ],
        scratch=[pltpu.VMEM((full, cells), jnp.bfloat16)],
    )
    mirror_in, cot_out = lax.optimization_barrier((mirror_in, cot_out))
    return (act_out[None], cot_out[None], mirror_in[None])


def solution(mesh):
    placed = (
        P("section", "ch", None),
        P("section", "ch", None),
        P("ch", None),
        P("ch", None),
        P("section", None, "ch", None),
        P("section", None, "ch", None),
        P("section", None, "ch", None),
        P(None, "ch"),
        P("section", None),
        P("section", None),
    )
    return jax.shard_map(
        local,
        mesh=mesh,
        in_specs=placed,
        out_specs=(P("section", "ch", None), P("section", "ch", None), P("section", "ch", None)),
        check_vma=False,
    )
```

```python
import jax
import jax.numpy as jnp
from jax import lax
from jax.experimental import pallas as pl
from jax.experimental.pallas import tpu as pltpu
from jax.sharding import PartitionSpec as P

C = 1280
GROUPS = 32
CELLS = 64
WIDTH = C // GROUPS

epsilon = 1e-05

VMEM = pl.BlockSpec(memory_space=pltpu.VMEM)
SMEM = pl.BlockSpec(memory_space=pltpu.SMEM)


def shifted(block, axis, distance):
    devices = range(lax.axis_size(axis))
    route = [(i - distance, i) for i in devices if i - distance in devices]
    return lax.ppermute(block, axis, route)


def swap_core(block):
    return lax.ppermute(block, "ch", [(0, 1), (1, 0), (2, 3), (3, 2)])


def swap_chip(block):
    return lax.ppermute(block, "ch", [(0, 2), (2, 0), (1, 3), (3, 1)])


def frame_shift(values, frames_by):
    step = frames_by * CELLS
    if step == 0:
        return values
    width = values.shape[1]
    lane = lax.broadcasted_iota(jnp.int32, values.shape, 1)
    rolled = pltpu.roll(values, (-step) % width, 1)
    kept = lane < width - step if step > 0 else lane >= -step
    return jnp.where(kept, rolled, 0.0)


def group_mean(grouped):
    total = jnp.sum(jnp.sum(grouped, axis=1, keepdims=True), axis=2, keepdims=True)
    return total * (1.0 / (grouped.shape[1] * grouped.shape[2]))


def by_group(values):
    return values.reshape(values.shape[0] // WIDTH, WIDTH, values.shape[1])


def normalize(values):
    grouped = by_group(values)
    centred = grouped - group_mean(grouped)
    factor = lax.rsqrt(group_mean(centred * centred) + epsilon)
    return (centred * factor).reshape(values.shape), factor


def column(table_ref, stamp):
    width = table_ref.shape[1]
    row = jnp.broadcast_to(table_ref[pl.ds(stamp, 1), :], (width, width))
    across = lax.broadcasted_iota(jnp.int32, (width, width), 0)
    along = lax.broadcasted_iota(jnp.int32, (width, width), 1)
    return jnp.sum(jnp.where(across == along, row, 0.0), axis=1, keepdims=True)


def transpose_kernel(weight_ref, out_ref):
    depth = weight_ref.shape[0]
    for start in range(0, depth, 128):
        size = min(128, depth - start)
        out_ref[:, start : start + size] = weight_ref[start : start + size, :].T


def forward_kernel(place_ref, arrived_ref, entry_ref, weight_ref, mate_ref, stacked_ref):
    rows = arrived_ref.shape[0]
    first = place_ref[0] == 0
    x_in = jnp.where(first, entry_ref[...], arrived_ref[...]).astype(jnp.float32)
    normed, _ = normalize(x_in)
    acted = normed / (1.0 + jnp.exp(-normed))
    for k in range(3):
        stacked_ref[k * rows : (k + 1) * rows, :] = frame_shift(acted, k - 1).astype(jnp.bfloat16)
    own_side(1 - place_ref[1], place_ref[2], weight_ref, stacked_ref, mate_ref)


def own_side(core, chip, weight_ref, stacked_ref, out_ref):
    rows = out_ref.shape[1]
    for side in range(2):
        block = jnp.bitwise_xor(chip, 1 - side) * 2 + core
        start = pl.multiple_of(block * rows, rows)
        out_ref[side] = jnp.dot(
            weight_ref[pl.ds(start, rows), :], stacked_ref[...], preferred_element_type=jnp.float32
        )


def own_kernel(place_ref, weight_ref, stacked_ref, own_ref):
    own_side(place_ref[1], place_ref[2], weight_ref, stacked_ref, own_ref)


def prepare_kernel(
    place_ref, plan_ref, stamps_ref, skip_ref, gain_ref, columns_ref, added_ref, extra_ref
):
    for way in range(2):
        columns_ref[way] = jnp.broadcast_to(
            column(gain_ref, stamps_ref[0, way]), columns_ref.shape[1:]
        )
    encoder = place_ref[4] == 1
    added = skip_ref[plan_ref[0, 0]]
    extra = skip_ref[plan_ref[0, 1]]
    added_ref[...] = jnp.where(encoder, jnp.zeros_like(added), added)
    extra_ref[...] = jnp.where(encoder, extra, jnp.zeros_like(extra))


def cotangent(place_ref, returned_ref, reward_ref, extra_ref):
    cot_in = jnp.where(place_ref[3] == 1, reward_ref[...], returned_ref[...])
    return cot_in.astype(jnp.float32) + extra_ref[...].astype(jnp.float32)


def scaled_kernel(place_ref, returned_ref, reward_ref, extra_ref, columns_ref, scaled_ref):
    cot_total = cotangent(place_ref, returned_ref, reward_ref, extra_ref)
    scaled_ref[...] = gained(cot_total, columns_ref, 1).astype(jnp.bfloat16)


def halves_kernel(own_ref, mate_ref, far_ref):
    far_ref[...] = (own_ref[0] + mate_ref[0]).astype(jnp.bfloat16)


def gained(values, columns_ref, way):
    size = columns_ref.shape[2]
    return jnp.concatenate(
        [
            values[:, start : start + size] * columns_ref[way]
            for start in range(0, values.shape[1], size)
        ],
        1,
    )


def near_kernel(
    place_ref,
    plan_ref,
    own_ref,
    mate_ref,
    arrived_ref,
    entry_ref,
    added_ref,
    columns_ref,
    stored_ref,
    near_ref,
    normed_ref,
    factor_ref,
    slope_ref,
):
    x_in = jnp.where(place_ref[0] == 0, entry_ref[...], arrived_ref[...]).astype(jnp.float32)
    near = gained(own_ref[1] + mate_ref[1], columns_ref, 0)
    near_ref[...] = x_in + near + added_ref[...].astype(jnp.float32)
    normed, factor = normalize(stored_ref[plan_ref[0, 1]].astype(jnp.float32))
    normed_ref[...] = normed
    factor_ref[...] = jnp.broadcast_to(factor, factor_ref.shape)
    sigmoid = 1.0 / (1.0 + jnp.exp(-normed))
    slope_ref[...] = sigmoid * (1.0 + normed * (1.0 - sigmoid))


def output_kernel(near_ref, far_ref, columns_ref, out_ref):
    far = gained(far_ref[...].astype(jnp.float32), columns_ref, 0)
    out_ref[...] = (near_ref[...] + far).astype(jnp.bfloat16)


def sent_kernel(place_ref, near_ref, far_ref, columns_ref, cot_ref, reward_ref, sent_ref):
    @pl.when(place_ref[4] == 1)
    def _():
        output_kernel(near_ref, far_ref, columns_ref, sent_ref)

    @pl.when(place_ref[5] == 1)
    def _():
        sent_ref[...] = reward_ref[...]

    @pl.when(place_ref[4] + place_ref[5] == 0)
    def _():
        sent_ref[...] = cot_ref[...]


def split_kernel(scaled_ref, other_ref, *part_refs):
    half = part_refs[0].shape[0]
    for i, part_ref in enumerate(part_refs):
        source_ref = (scaled_ref, other_ref)[i // 2]
        part_ref[...] = source_ref[i % 2 * half : (i % 2 + 1) * half, :]


def gradient_kernel(
    place_ref,
    normed_ref,
    factor_ref,
    slope_ref,
    returned_ref,
    reward_ref,
    extra_ref,
    scaled_ref,
    other_ref,
    mate_low_ref,
    mate_high_ref,
    other_low_ref,
    other_high_ref,
    weight_ref,
    out_ref,
    whole_ref,
):
    rows = scaled_ref.shape[0]
    core, chip = place_ref[1], place_ref[2]

    def put(chip, core, block, skipped=0):
        start = pl.multiple_of((chip * 2 + core) * rows + skipped, 32)
        whole_ref[pl.ds(start, block.shape[0]), :] = block

    put(chip, core, scaled_ref[...])
    put(1 - chip, core, other_ref[...])
    put(chip, 1 - core, mate_low_ref[...])
    put(chip, 1 - core, mate_high_ref[...], rows // 2)
    put(1 - chip, 1 - core, other_low_ref[...])
    put(1 - chip, 1 - core, other_high_ref[...], rows // 2)
    cot_total = cotangent(place_ref, returned_ref, reward_ref, extra_ref)
    normed = normed_ref[...]
    folded = jnp.dot(weight_ref[...], whole_ref[...], preferred_element_type=jnp.float32)
    d_acted = (
        frame_shift(folded[:rows], 1)
        + folded[rows : 2 * rows]
        + frame_shift(folded[2 * rows :], -1)
    )
    d_normed = by_group(d_acted * slope_ref[...])
    grouped = by_group(normed)
    result = factor_ref[:, :1, :1] * (
        d_normed - group_mean(d_normed) - grouped * group_mean(d_normed * grouped)
    )
    out_ref[...] = (cot_total + result.reshape(cot_total.shape)).astype(jnp.bfloat16)


def call(kernel, outs, specs, args, scratch=(), cost=0.0, limit=16):
    return pl.pallas_call(
        kernel,
        out_shape=[jax.ShapeDtypeStruct(shape, kind) for shape, kind in outs],
        in_specs=specs,
        out_specs=[VMEM] * len(outs),
        scratch_shapes=list(scratch),
        compiler_params=pltpu.CompilerParams(vmem_limit_bytes=limit * 2**20),
        cost_estimate=pl.CostEstimate(
            flops=int(cost * 1e9), bytes_accessed=int(cost * 1e6), transcendentals=0
        ),
        name=kernel.__name__,
    )(*args)


def local(
    act_carried,
    cot_carried,
    entry_latent,
    reward_head,
    stored_inputs,
    skip_buffer,
    conv_weight,
    time_gain,
    plan,
    timesteps,
):
    sections = lax.axis_size("section")
    section = lax.axis_index("section")
    ch = lax.axis_index("ch")
    rows, cells = act_carried.shape[1:]
    weight = conv_weight[0].reshape(3 * rows, -1)
    full = weight.shape[1]
    stored, skips = stored_inputs[0], skip_buffer[0]
    last = (section == sections - 1).astype(jnp.int32)
    encoder = (section < sections // 2).astype(jnp.int32)
    middle = (section == sections // 2).astype(jnp.int32)
    place = jnp.stack([section, ch % 2, ch // 2, last, encoder, middle])
    field = ((rows, cells), jnp.bfloat16)
    pair = ((2, rows, cells), jnp.float32)

    arrived = shifted(act_carried[0], "section", 1)
    (turned,) = call(transpose_kernel, [((full, 3 * rows), jnp.bfloat16)], [VMEM], [weight], cost=20.0)
    turned, skips, time_gain = lax.optimization_barrier((turned, skips, time_gain))
    gains, added, extra = call(
        prepare_kernel,
        [((2, rows, 128), jnp.float32), field, field],
        [SMEM] * 3 + [VMEM] * 2,
        [place, plan, timesteps, skips, time_gain],
        cost=20.0,
    )
    cotangents, gains, turned = lax.optimization_barrier((cot_carried[0], gains, turned))
    returned = shifted(cotangents, "section", -1)

    mate_side, stacked = call(
        forward_kernel,
        [pair, ((3 * rows, cells), jnp.bfloat16)],
        [SMEM, VMEM, VMEM, VMEM],
        [place, arrived, entry_latent, turned],
    )
    mate_part = swap_core(mate_side)
    (own,) = call(own_kernel, [pair], [SMEM, VMEM, VMEM], [place, turned, stacked], cost=20.0)
    (far_side,) = call(halves_kernel, [field], [VMEM, VMEM], [own, mate_part])
    far = swap_chip(far_side)
    stored, far_side = lax.optimization_barrier((stored, far_side))
    whole = ((rows, cells), jnp.float32)
    near, saved_normed, saved_factor, slope = call(
        near_kernel,
        [whole, whole, ((rows // WIDTH, 8, 128), jnp.float32), whole],
        [SMEM] * 2 + [VMEM] * 7,
        [place, plan, own, mate_part, arrived, entry_latent, added, gains, stored],
        cost=20.0,
    )
    returned, near = lax.optimization_barrier((returned, near))
    (scaled,) = call(
        scaled_kernel,
        [field],
        [SMEM] + [VMEM] * 4,
        [place, returned, reward_head, extra, gains],
    )
    other = swap_chip(scaled)
    far, scaled = lax.optimization_barrier((far, scaled))
    (sent,) = call(
        sent_kernel,
        [field],
        [SMEM] + [VMEM] * 5,
        [place, near, far, gains, cot_carried[0], reward_head],
    )
    half = sections // 2
    route = [(s, sections - 1 - s) for s in range(half)]
    route += [(s, (sections - s) % half) for s in range(half, sections)]
    mirror_in = lax.ppermute(sent, "section", route)

    other, scaled, near, sent = lax.optimization_barrier((other, scaled, near, sent))
    (act_out,) = call(output_kernel, [field], [VMEM] * 3, [near, far, gains])
    parts = call(
        split_kernel,
        [((rows // 2, cells), jnp.bfloat16)] * 4,
        [VMEM] * 2,
        [scaled, other],
    )
    mates = [swap_core(part) for part in parts]
    (cot_out,) = call(
        gradient_kernel,
        [field],
        [SMEM] + [VMEM] * 13,
        [
            place,
            saved_normed,
            saved_factor,
            slope,
            returned,
            reward_head,
            extra,
            scaled,
            other,
            *mates,
            weight,
        ],
        scratch=[pltpu.VMEM((full, cells), jnp.bfloat16)],
    )
    mirror_in, cot_out = lax.optimization_barrier((mirror_in, cot_out))
    return (act_out[None], cot_out[None], mirror_in[None])


def solution(mesh):
    placed = (
        P("section", "ch", None),
        P("section", "ch", None),
        P("ch", None),
        P("ch", None),
        P("section", None, "ch", None),
        P("section", None, "ch", None),
        P("section", None, "ch", None),
        P(None, "ch"),
        P("section", None),
        P("section", None),
    )
    return jax.shard_map(
        local,
        mesh=mesh,
        in_specs=placed,
        out_specs=(P("section", "ch", None), P("section", "ch", None), P("section", "ch", None)),
        check_vma=False,
    )
```

```python
import jax
import jax.numpy as jnp
from jax import lax
from jax.experimental import pallas as pl
from jax.experimental.pallas import tpu as pltpu
from jax.sharding import PartitionSpec as P

C = 1280
GROUPS = 32
CELLS = 64
WIDTH = C // GROUPS

epsilon = 1e-05

VMEM = pl.BlockSpec(memory_space=pltpu.VMEM)
SMEM = pl.BlockSpec(memory_space=pltpu.SMEM)


def shifted(block, axis, distance):
    devices = range(lax.axis_size(axis))
    route = [(i - distance, i) for i in devices if i - distance in devices]
    return lax.ppermute(block, axis, route)


def swap_core(block):
    return lax.ppermute(block, "ch", [(0, 1), (1, 0), (2, 3), (3, 2)])


def swap_chip(block):
    return lax.ppermute(block, "ch", [(0, 2), (2, 0), (1, 3), (3, 1)])


def frame_shift(values, frames_by):
    step = frames_by * CELLS
    if step == 0:
        return values
    width = values.shape[1]
    lane = lax.broadcasted_iota(jnp.int32, values.shape, 1)
    rolled = pltpu.roll(values, (-step) % width, 1)
    kept = lane < width - step if step > 0 else lane >= -step
    return jnp.where(kept, rolled, 0.0)


def group_mean(grouped):
    total = jnp.sum(jnp.sum(grouped, axis=1, keepdims=True), axis=2, keepdims=True)
    return total * (1.0 / (grouped.shape[1] * grouped.shape[2]))


def by_group(values):
    return values.reshape(values.shape[0] // WIDTH, WIDTH, values.shape[1])


def normalize(values):
    grouped = by_group(values)
    centred = grouped - group_mean(grouped)
    factor = lax.rsqrt(group_mean(centred * centred) + epsilon)
    return (centred * factor).reshape(values.shape), factor


def column(table_ref, stamp):
    width = table_ref.shape[1]
    row = jnp.broadcast_to(table_ref[pl.ds(stamp, 1), :], (width, width))
    across = lax.broadcasted_iota(jnp.int32, (width, width), 0)
    along = lax.broadcasted_iota(jnp.int32, (width, width), 1)
    return jnp.sum(jnp.where(across == along, row, 0.0), axis=1, keepdims=True)


def transpose_kernel(weight_ref, out_ref):
    depth = weight_ref.shape[0]
    for start in range(0, depth, 128):
        size = min(128, depth - start)
        out_ref[:, start : start + size] = weight_ref[start : start + size, :].T


def forward_kernel(place_ref, arrived_ref, entry_ref, weight_ref, mate_ref, stacked_ref):
    rows = arrived_ref.shape[0]
    first = place_ref[0] == 0
    x_in = jnp.where(first, entry_ref[...], arrived_ref[...]).astype(jnp.float32)
    normed, _ = normalize(x_in)
    acted = (normed / (1.0 + jnp.exp(-normed))).astype(jnp.bfloat16)
    empty = jnp.zeros((rows, CELLS), jnp.bfloat16)
    stacked_ref[:rows, :] = jnp.concatenate([empty, acted[:, :-CELLS]], 1)
    stacked_ref[rows : 2 * rows, :] = acted
    stacked_ref[2 * rows :, :] = jnp.concatenate([acted[:, CELLS:], empty], 1)
    own_side(1 - place_ref[1], place_ref[2], weight_ref, stacked_ref, mate_ref)


def own_side(core, chip, weight_ref, stacked_ref, out_ref):
    rows = out_ref.shape[1]
    for side in range(2):
        block = jnp.bitwise_xor(chip, 1 - side) * 2 + core
        start = pl.multiple_of(block * rows, rows)
        out_ref[side] = jnp.dot(
            weight_ref[pl.ds(start, rows), :], stacked_ref[...], preferred_element_type=jnp.float32
        )


def own_kernel(place_ref, weight_ref, stacked_ref, own_ref):
    own_side(place_ref[1], place_ref[2], weight_ref, stacked_ref, own_ref)


def prepare_kernel(place_ref, plan_ref, stamps_ref, skip_ref, gain_ref, columns_ref, added_ref):
    spread(gain_ref, stamps_ref[0, 0], columns_ref)
    added = skip_ref[plan_ref[0, 0]]
    added_ref[...] = jnp.where(place_ref[4] == 1, jnp.zeros_like(added), added)


def spread(gain_ref, stamp, columns_ref):
    columns_ref[...] = jnp.broadcast_to(column(gain_ref, stamp), columns_ref.shape)


def cotangent(place_ref, returned_ref, reward_ref, extra_ref):
    cot_in = jnp.where(place_ref[3] == 1, reward_ref[...], returned_ref[...])
    return cot_in.astype(jnp.float32) + extra_ref[...].astype(jnp.float32)


def scaled_kernel(place_ref, returned_ref, reward_ref, extra_ref, columns_ref, scaled_ref):
    cot_total = cotangent(place_ref, returned_ref, reward_ref, extra_ref)
    scaled_ref[...] = gained(cot_total, columns_ref).astype(jnp.bfloat16)


def halves_kernel(own_ref, mate_ref, far_ref, after_ref):
    after_ref[...] = jnp.zeros_like(after_ref)
    far_ref[...] = (own_ref[0] + mate_ref[0]).astype(jnp.bfloat16)


def gained(values, columns_ref):
    size = columns_ref.shape[1]
    return jnp.concatenate(
        [
            values[:, start : start + size] * columns_ref[...]
            for start in range(0, values.shape[1], size)
        ],
        1,
    )


def near_kernel(
    place_ref,
    after_ref,
    own_ref,
    mate_ref,
    arrived_ref,
    entry_ref,
    added_ref,
    columns_ref,
    near_ref,
):
    x_in = jnp.where(place_ref[0] == 0, entry_ref[...], arrived_ref[...]).astype(jnp.float32)
    near = gained(own_ref[1] + mate_ref[1], columns_ref)
    near_ref[...] = x_in + near + added_ref[...].astype(jnp.float32)


def saved_kernel(plan_ref, after_ref, stored_ref, normed_ref, factor_ref, slope_ref):
    normed, factor = normalize(stored_ref[plan_ref[0, 1]].astype(jnp.float32))
    normed_ref[...] = normed
    factor_ref[...] = jnp.broadcast_to(factor, factor_ref.shape)
    sigmoid = 1.0 / (1.0 + jnp.exp(-normed))
    slope_ref[...] = sigmoid * (1.0 + normed * (1.0 - sigmoid))


def back_kernel(
    place_ref, plan_ref, stamps_ref, after_ref, skip_ref, gain_ref, extra_ref, back_ref
):
    spread(gain_ref, stamps_ref[0, 1], back_ref)
    extra = skip_ref[plan_ref[0, 1]]
    extra_ref[...] = jnp.where(place_ref[4] == 1, extra, jnp.zeros_like(extra))


def output_kernel(near_ref, far_ref, columns_ref, out_ref):
    far = gained(far_ref[...].astype(jnp.float32), columns_ref)
    out_ref[...] = (near_ref[...] + far).astype(jnp.bfloat16)


def sent_kernel(place_ref, near_ref, far_ref, columns_ref, cot_ref, reward_ref, sent_ref):
    @pl.when(place_ref[4] == 1)
    def _():
        output_kernel(near_ref, far_ref, columns_ref, sent_ref)

    @pl.when(place_ref[5] == 1)
    def _():
        sent_ref[...] = reward_ref[...]

    @pl.when(place_ref[4] + place_ref[5] == 0)
    def _():
        sent_ref[...] = cot_ref[...]


def split_kernel(scaled_ref, other_ref, *part_refs):
    half = part_refs[0].shape[0]
    for i, part_ref in enumerate(part_refs):
        source_ref = (scaled_ref, other_ref)[i // 2]
        part_ref[...] = source_ref[i % 2 * half : (i % 2 + 1) * half, :]


def gradient_kernel(
    place_ref,
    normed_ref,
    factor_ref,
    slope_ref,
    returned_ref,
    reward_ref,
    extra_ref,
    scaled_ref,
    other_ref,
    mate_low_ref,
    mate_high_ref,
    other_low_ref,
    other_high_ref,
    weight_ref,
    out_ref,
    whole_ref,
):
    rows = scaled_ref.shape[0]
    core, chip = place_ref[1], place_ref[2]

    def put(chip, core, block, skipped=0):
        start = pl.multiple_of((chip * 2 + core) * rows + skipped, 32)
        whole_ref[pl.ds(start, block.shape[0]), :] = block

    put(chip, core, scaled_ref[...])
    put(1 - chip, core, other_ref[...])
    put(chip, 1 - core, mate_low_ref[...])
    put(chip, 1 - core, mate_high_ref[...], rows // 2)
    put(1 - chip, 1 - core, other_low_ref[...])
    put(1 - chip, 1 - core, other_high_ref[...], rows // 2)
    cot_total = cotangent(place_ref, returned_ref, reward_ref, extra_ref)
    normed = normed_ref[...]
    folded = jnp.dot(weight_ref[...], whole_ref[...], preferred_element_type=jnp.float32)
    d_acted = (
        frame_shift(folded[:rows], 1)
        + folded[rows : 2 * rows]
        + frame_shift(folded[2 * rows :], -1)
    )
    d_normed = by_group(d_acted * slope_ref[...])
    grouped = by_group(normed)
    result = factor_ref[:, :1, :1] * (
        d_normed - group_mean(d_normed) - grouped * group_mean(d_normed * grouped)
    )
    out_ref[...] = (cot_total + result.reshape(cot_total.shape)).astype(jnp.bfloat16)


def call(kernel, outs, specs, args, scratch=(), cost=0.0, limit=16):
    return pl.pallas_call(
        kernel,
        out_shape=[jax.ShapeDtypeStruct(shape, kind) for shape, kind in outs],
        in_specs=specs,
        out_specs=[VMEM] * len(outs),
        scratch_shapes=list(scratch),
        compiler_params=pltpu.CompilerParams(vmem_limit_bytes=limit * 2**20),
        cost_estimate=pl.CostEstimate(
            flops=int(cost * 1e9), bytes_accessed=int(cost * 1e6), transcendentals=0
        ),
        name=kernel.__name__,
    )(*args)


def local(
    act_carried,
    cot_carried,
    entry_latent,
    reward_head,
    stored_inputs,
    skip_buffer,
    conv_weight,
    time_gain,
    plan,
    timesteps,
):
    sections = lax.axis_size("section")
    section = lax.axis_index("section")
    ch = lax.axis_index("ch")
    rows, cells = act_carried.shape[1:]
    weight = conv_weight[0].reshape(3 * rows, -1)
    full = weight.shape[1]
    stored, skips = stored_inputs[0], skip_buffer[0]
    last = (section == sections - 1).astype(jnp.int32)
    encoder = (section < sections // 2).astype(jnp.int32)
    middle = (section == sections // 2).astype(jnp.int32)
    place = jnp.stack([section, ch % 2, ch // 2, last, encoder, middle])
    field = ((rows, cells), jnp.bfloat16)
    pair = ((2, rows, cells), jnp.float32)

    arrived = shifted(act_carried[0], "section", 1)
    (turned,) = call(transpose_kernel, [((full, 3 * rows), jnp.bfloat16)], [VMEM], [weight], cost=20.0)
    turned, skips, time_gain = lax.optimization_barrier((turned, skips, time_gain))
    column_kind = ((rows, 128), jnp.float32)
    gains, added = call(
        prepare_kernel,
        [column_kind, field],
        [SMEM] * 3 + [VMEM] * 2,
        [place, plan, timesteps, skips, time_gain],
        cost=20.0,
    )
    cotangents, gains, turned = lax.optimization_barrier((cot_carried[0], gains, turned))
    returned = shifted(cotangents, "section", -1)

    mate_side, stacked = call(
        forward_kernel,
        [pair, ((3 * rows, cells), jnp.bfloat16)],
        [SMEM, VMEM, VMEM, VMEM],
        [place, arrived, entry_latent, turned],
    )
    mate_part = swap_core(mate_side)
    (own,) = call(own_kernel, [pair], [SMEM, VMEM, VMEM], [place, turned, stacked], cost=20.0)
    far_side, after = call(
        halves_kernel, [field, ((8, 128), jnp.float32)], [VMEM, VMEM], [own, mate_part]
    )
    far = swap_chip(far_side)
    whole = ((rows, cells), jnp.float32)
    (near,) = call(
        near_kernel,
        [whole],
        [SMEM] + [VMEM] * 7,
        [place, after, own, mate_part, arrived, entry_latent, added, gains],
    )
    saved_normed, saved_factor, slope = call(
        saved_kernel,
        [whole, ((rows // WIDTH, 8, 128), jnp.float32), whole],
        [SMEM] + [VMEM] * 2,
        [plan, after, stored],
        cost=20.0,
    )
    extra, back_gains = call(
        back_kernel,
        [field, column_kind],
        [SMEM] * 3 + [VMEM] * 3,
        [place, plan, timesteps, after, skips, time_gain],
    )
    returned, near, slope = lax.optimization_barrier((returned, near, slope))
    (scaled,) = call(
        scaled_kernel,
        [field],
        [SMEM] + [VMEM] * 4,
        [place, returned, reward_head, extra, back_gains],
    )
    other = swap_chip(scaled)
    far, scaled = lax.optimization_barrier((far, scaled))
    (sent,) = call(
        sent_kernel,
        [field],
        [SMEM] + [VMEM] * 5,
        [place, near, far, gains, cot_carried[0], reward_head],
    )
    half = sections // 2
    route = [(s, sections - 1 - s) for s in range(half)]
    route += [(s, (sections - s) % half) for s in range(half, sections)]
    mirror_in = lax.ppermute(sent, "section", route)

    other, scaled, near, sent = lax.optimization_barrier((other, scaled, near, sent))
    (act_out,) = call(output_kernel, [field], [VMEM] * 3, [near, far, gains])
    parts = call(
        split_kernel,
        [((rows // 2, cells), jnp.bfloat16)] * 4,
        [VMEM] * 2,
        [scaled, other],
    )
    mates = [swap_core(part) for part in parts]
    (cot_out,) = call(
        gradient_kernel,
        [field],
        [SMEM] + [VMEM] * 13,
        [
            place,
            saved_normed,
            saved_factor,
            slope,
            returned,
            reward_head,
            extra,
            scaled,
            other,
            *mates,
            weight,
        ],
        scratch=[pltpu.VMEM((full, cells), jnp.bfloat16)],
    )
    mirror_in, cot_out = lax.optimization_barrier((mirror_in, cot_out))
    return (act_out[None], cot_out[None], mirror_in[None])


def solution(mesh):
    placed = (
        P("section", "ch", None),
        P("section", "ch", None),
        P("ch", None),
        P("ch", None),
        P("section", None, "ch", None),
        P("section", None, "ch", None),
        P("section", None, "ch", None),
        P(None, "ch"),
        P("section", None),
        P("section", None),
    )
    return jax.shard_map(
        local,
        mesh=mesh,
        in_specs=placed,
        out_specs=(P("section", "ch", None), P("section", "ch", None), P("section", "ch", None)),
        check_vma=False,
    )
```
